256 devices in a mesh: loop: 64 (over y, x_hi, z), layer: 4 (over x_lo, core).
Axes of the slice: x: 4 (x_hi: 2, x_lo: 2; x = x_hi * 2 + x_lo), y: 4, z: 8, core: 2. Of those that a mesh axis runs over, the one named last changes fastest.
Arguments:
- queries: bfloat16 [8192, 768], P('loop'), may hold values from -8 to 8, as said below
- candidates: bfloat16 [32768, 768], P(('loop', 'layer')), may hold values from -8 to 8, as said below
- cand_ids: int32 [32768], P(('loop', 'layer')), may hold values from 0 to 32767, each once
Outputs:
- near_dist: float32 [8192, 32], P(('loop', 'layer'))
- near_ids: int32 [8192, 32], P(('loop', 'layer'))
The draws below stay inside these ranges and needn't reach their ends.
Inputs may be any that keep to these rules, and one draw needn't show every extreme that they name: `queries`: every entry is a whole number. `candidates`: every entry is a whole number.
All inputs are finite; a program needn't handle non-finite values.
Results may differ from the reference program's by a relative error of at most 0.0003.
Values may be sent and summed in bfloat16 or wider, within the bound.
A program may use at most 64 MiB of HBM per device.

```python
import jax
import jax.numpy as jnp
from jax import lax

D = 768
K = 32
STEPS = 4
QDEV = 128
CB = 128
NQ = 8192
NC = 32768
N_LOOP = 64
N_LAYER = 4


def whole_values(key, rows):
    values = jax.random.randint(key, (rows, D), -3, 5)
    return values.astype(jnp.float32)


def draw_queries(key, part):
    key = jax.random.fold_in(key, 11)
    return whole_values(key, NQ).astype(jnp.bfloat16)


def draw_candidates(key, part):
    key = jax.random.fold_in(key, 23)
    return whole_values(key, NC).astype(jnp.bfloat16)


def setup_inputs(seed: int = 0) -> dict:
    arg_keys = jax.random.split(jax.random.key(seed), 4)
    queries = draw_queries(jax.random.fold_in(arg_keys[3], 71), 0)
    candidates = draw_candidates(jax.random.fold_in(arg_keys[3], 71), 0)
    cand_ids = jax.random.permutation(arg_keys[2], NC).astype(jnp.int32)
    return {"queries": queries, "candidates": candidates, "cand_ids": cand_ids}


def select(dist, ids, count):
    ordered = lax.sort((dist, ids), dimension=1, num_keys=2)
    return ordered[0][:, :count], ordered[1][:, :count]


def order_list(dist, ids):
    return lax.sort((dist, ids), dimension=1, num_keys=2)


def reference(queries, candidates, cand_ids):
    groups = candidates.reshape(N_LOOP, N_LAYER * CB, D)
    group_ids = cand_ids.reshape(N_LOOP, N_LAYER * CB)
    shards = queries.reshape(N_LOOP, QDEV, D)

    def one_shard(index):
        picks = (index - jnp.arange(STEPS + 1, dtype=jnp.int32)) % N_LOOP
        chosen = groups[picks].reshape(-1, D)
        chosen_ids = group_ids[picks].reshape(-1)
        block = shards[index]
        query_norm = jnp.sum(jnp.square(block.astype(jnp.float32)), 1)
        cand_norm = jnp.sum(jnp.square(chosen.astype(jnp.float32)), 1)
        inner = jnp.dot(block, chosen.T, preferred_element_type=jnp.float32)
        dist = query_norm[:, None] + cand_norm[None, :] - 2.0 * inner
        every_id = jnp.broadcast_to(chosen_ids[None, :], dist.shape)
        kept, kept_ids = select(dist, every_id, K)
        return order_list(kept, kept_ids)

    dists, idents = lax.map(one_shard, jnp.arange(N_LOOP, dtype=jnp.int32))
    scale = 0.125 / D
    return dists.reshape(NQ, K) * scale, idents.reshape(NQ, K)
```

```python
import jax
import jax.numpy as jnp
from jax import lax
from jax.experimental import pallas as pl
from jax.experimental.pallas import tpu as pltpu
from jax.sharding import PartitionSpec as P

D = 768
K = 32
STEPS = 4
LOOP = 64
ROW = 8
LAYERS = 4
CB = 128
ROWS = 32
RELAY = 5
CHUNKS = 2
PIECE = ROWS // CHUNKS
CAND_CHUNKS = 2
CAND_PIECE = CB // CAND_CHUNKS
MESH = pl.DeviceIdType.MESH
NT = (((1,), (1,)), ((), ()))


def batcher(count):
    pairs = []
    p = 1
    while p < count:
        k = p
        while k >= 1:
            for j in range(k % p, count - k, 2 * k):
                for i in range(min(k, count - j - k)):
                    if (i + j) // (2 * p) == (i + j + k) // (2 * p):
                        pairs.append((i + j, i + j + k))
            k //= 2
        p *= 2
    return pairs


SORT16 = batcher(16)


def exchange(values, low, high):
    a, b = values[low], values[high]
    values[low], values[high] = jnp.minimum(a, b), jnp.maximum(a, b)


def settle(values):
    for gap in (8, 4, 2, 1):
        for k in range(16):
            if not k & gap:
                exchange(values, k, k + gap)


def smallest(key):
    row = lax.broadcasted_iota(jnp.int32, (8, 128), 0)
    upper = row >= 4
    v = [key[8 * g : 8 * g + 8, :] for g in range(16)]
    for low, high in SORT16:
        exchange(v, low, high)
    r = [pltpu.roll(v[15 - k], 4, 0) for k in range(16)]
    v = [jnp.where(upper, jnp.maximum(v[k], r[k]), jnp.minimum(v[k], r[k])) for k in range(16)]
    settle(v)
    for shift, lanes in ((2, 0), (3, 0), (4, 96), (4, 64)):
        r = [pltpu.roll(v[15 - k], shift, 0) for k in range(16)]
        if lanes:
            r = [pltpu.roll(x, lanes, 1) for x in r]
        v = [jnp.minimum(v[k], r[k]) for k in range(16)]
        r = [pltpu.roll(x, 4, 0) for x in v]
        v = [jnp.where(upper, jnp.maximum(v[k], r[k]), jnp.minimum(v[k], r[k])) for k in range(16)]
        settle(v)
    return v


def by_layer(parts):
    group = lax.broadcasted_iota(jnp.int32, parts[0].shape, 1) // ROWS
    return jnp.where(
        group < 2, jnp.where(group == 0, parts[0], parts[1]), jnp.where(group == 2, parts[2], parts[3])
    )


def merged(first, second):
    place = lax.broadcasted_iota(jnp.int32, (K, 128), 0)

    def before(a, b):
        return (a[0] < b[0]) | ((a[0] == b[0]) & (a[1] < b[1]))

    lower = before(first, second)
    now = [jnp.where(lower, a, b) for a, b in zip(first, second)]
    for gap in (16, 8, 4, 2, 1):
        head = (place & gap) == 0
        other = [jnp.where(head, pltpu.roll(x, K - gap, 0), pltpu.roll(x, gap, 0)) for x in now]
        keep = before(now, other) == head
        now = [jnp.where(keep, a, b) for a, b in zip(now, other)]
    return now


def kernel(
    q_ref, c_ref, id_ref, dist_ref, near_ref,
    slots, cands, idents, base, table, keys, mine, outbox, inbox,
    local_sem, slot_send, slot_recv, relay_send, cand_send, cand_recv, id_send, id_recv, res_send, res_recv, ring_sem,
):
    i, l = lax.axis_index("loop"), lax.axis_index("layer")
    z = lax.rem(i, ROW)

    def at(offset):
        return (lax.rem(i + offset + 2 * LOOP, LOOP), l)

    def remote(src, dst, send, recv, device):
        return pltpu.make_async_remote_copy(
            src_ref=src, dst_ref=dst, send_sem=send, recv_sem=recv, device_id=device, device_id_type=MESH
        )

    own_q = pltpu.make_async_copy(q_ref.at[pl.ds(l * ROWS, ROWS)], slots.at[0], local_sem.at[0])
    own_c = pltpu.make_async_copy(c_ref, cands.at[l], local_sem.at[1])
    own_id = pltpu.make_async_copy(id_ref, idents.at[l], local_sem.at[2])
    own_q.start()
    own_id.start()
    own_c.start()

    barrier = pltpu.get_barrier_semaphore()

    def hello(device):
        pl.semaphore_signal(barrier, inc=1, device_id=device, device_id_type=MESH)

    @pl.when(z == 0)
    def _():
        for k in range(4):
            hello(at(ROW + k))
        hello(at(ROW - 1))

    @pl.when(z < ROW - 1)
    def _():
        hello(at(1))

    for k in (1, 2, 3):
        hello((i, l ^ k))
    own_q.wait()
    own_id.wait()
    own_c.wait()
    extra = jnp.where((z >= 1) & (z <= 3), 1, 0) + jnp.where(z == ROW - 1, 1, 0)
    pl.semaphore_wait(barrier, 4 + extra)

    first = jnp.where(z == 0, RELAY, 0)
    below = at(jnp.where(z == 0, ROW - 1, -1))

    def slot_copy(source, target, chunk, device):
        rows = pl.ds(chunk * PIECE, PIECE)
        return remote(
            slots.at[source, rows], slots.at[target, rows],
            slot_send.at[target, chunk], slot_recv.at[target, chunk], device,
        )

    def relay_copy(chunk):
        rows = pl.ds(chunk * PIECE, PIECE)
        return remote(
            slots.at[0, rows], slots.at[RELAY + z, rows],
            relay_send.at[chunk], slot_recv.at[RELAY + z, chunk], at(-z - ROW),
        )

    def arrived(slot, chunk):
        rows = pl.ds(chunk * PIECE, PIECE)
        remote(
            slots.at[0, rows], slots.at[slot, rows], slot_send.at[1, chunk], slot_recv.at[slot, chunk], below
        ).wait_recv()

    def pass_on(s, chunk):
        slot_copy(first + s, s + 1, chunk, below).start()

    @pl.when(z < 4)
    def _():
        for chunk in range(CHUNKS):
            relay_copy(chunk).start()

    @pl.when(z == ROW - 1)
    def _():
        pl.semaphore_signal(ring_sem, inc=1, device_id=at(1 - ROW), device_id_type=MESH)

    @pl.when(z > 0)
    def _():
        for chunk in range(CHUNKS):
            pass_on(0, chunk)

    def cand_copy(block, chunk, kind, device):
        rows = pl.ds(chunk * CAND_PIECE, CAND_PIECE)
        return remote(
            cands.at[block, rows], cands.at[block, rows],
            cand_send.at[kind, chunk], cand_recv.at[kind, chunk], device,
        )

    def id_copy(k, block):
        return remote(
            idents.at[block], idents.at[block], id_send.at[k - 1], id_recv.at[k - 1], (i, l ^ k)
        )

    for k in (1, 2, 3):
        id_copy(k, l).start()
    for chunk in range(CAND_CHUNKS):
        cand_copy(l, chunk, 1, (i, l ^ 2)).start()
    for chunk in range(CAND_CHUNKS):
        cand_copy(l, chunk, 0, (i, l ^ 1)).start()

    for k in (1, 2, 3):
        id_copy(k, l ^ k).wait_recv()
    lane = lax.broadcasted_iota(jnp.int32, (CB, 128), 1)
    id_rows = [idents[m].astype(jnp.float32) for m in range(LAYERS)]
    id_cols = jnp.concatenate([jnp.broadcast_to(x, (ROWS, CB)) for x in id_rows], 0).T
    part = jnp.zeros((CB, 128), jnp.float32)
    for m in range(LAYERS):
        for k in range(4):
            shifted = pltpu.roll(jnp.broadcast_to(id_rows[m], (8, 128)), 32 * k, 1)[:1]
            part += jnp.where(shifted < id_cols, 1.0, 0.0)
    same = lax.broadcasted_iota(jnp.int32, (128, 128), 0) // ROWS == (
        lax.broadcasted_iota(jnp.int32, (128, 128), 1) // ROWS
    )
    rank = jnp.dot(
        part.astype(jnp.bfloat16),
        jnp.where(same, 1.0, 0.0).astype(jnp.bfloat16),
        preferred_element_type=jnp.float32,
    ).astype(jnp.int32)
    for a in range(4):
        total = jnp.zeros((1, 128), jnp.float32)
        for m in range(LAYERS):
            column = rank[:, ROWS * m : ROWS * m + 1]
            ident = id_cols[:, ROWS * m : ROWS * m + 1]
            total += jnp.sum(jnp.where(column == lane + 128 * a, ident, 0.0), 0, keepdims=True)
        table[a] = jnp.broadcast_to(total, (8, 128)).astype(jnp.int32)

    def cand_forward(chunk):
        cand_copy(l ^ 2, chunk, 1, (i, l ^ 2)).wait_recv()
        cand_copy(l ^ 2, chunk, 2, (i, l ^ 1)).start()

    @pl.when(z == 0)
    def _():
        for chunk in range(CAND_CHUNKS):
            cand_forward(chunk)
        pl.semaphore_wait(ring_sem, 1)
        for s in range(4):
            for chunk in range(CHUNKS):
                arrived(RELAY + s, chunk)
                pass_on(s, chunk)

    @pl.when(z > 0)
    def _():
        for s in (1, 2, 3):
            for chunk in range(CHUNKS):
                arrived(s, chunk)
                pass_on(s, chunk)
            if s <= CAND_CHUNKS:
                cand_forward(s - 1)

    for chunk in range(CAND_CHUNKS):
        cand_copy(l ^ 1, chunk, 0, (i, l ^ 1)).wait_recv()
    for chunk in range(CAND_CHUNKS):
        cand_copy(l ^ 3, chunk, 2, (i, l ^ 1)).wait_recv()

    ones = jnp.ones((128, D), jnp.bfloat16)
    norms = []
    for m in range(LAYERS):
        block = cands[m]
        norms.append(lax.dot_general(block * block, ones, NT, preferred_element_type=jnp.float32))
    base[...] = by_layer(norms).astype(jnp.int32) * 512 + rank

    start = jnp.where(z >= 4, ROW - z, 1)

    def result_copy(s):
        return remote(
            outbox.at[s], inbox.at[s - 1], res_send.at[s - 1], res_recv.at[s - 1], at(s)
        )

    def step(t, carry):
        s = lax.rem(start + t, STEPS + 1)

        @pl.when((s == 4) | ((z == 0) & (s > 0)))
        def _():
            for chunk in range(CHUNKS):
                arrived(s, chunk)

        block = slots[s]
        four = jnp.concatenate([block] * 4, 0)
        inner = by_layer(
            [lax.dot_general(cands[m], four, NT, preferred_element_type=jnp.float32) for m in range(LAYERS)]
        )
        v = smallest(base[...] - inner.astype(jnp.int32) * 1024)

        @pl.when(s == 0)
        def _():
            for k in range(16):
                keys[k : k + 1, :] = v[k][0:1, :]
                keys[16 + k : 17 + k, :] = v[k][4:5, :]

        @pl.when(s > 0)
        def _():
            for k in range(16):
                keys[31 - k : 32 - k, :] = v[k][0:1, :]
                keys[15 - k : 16 - k, :] = v[k][4:5, :]

        left = lax.broadcasted_iota(jnp.int32, (8, 128), 1) < ROWS
        for g in range(4):
            key = keys[8 * g : 8 * g + 8, :]
            place = key & 127
            which = (key >> 7) & 3
            found = [jnp.take_along_axis(table[a], place, axis=1, mode="promise_in_bounds") for a in range(4)]
            ident = jnp.where(
                which < 2, jnp.where(which == 0, found[0], found[1]), jnp.where(which == 2, found[2], found[3])
            )
            outbox[s, 8 * g : 8 * g + 8, :] = jnp.where(left, key >> 9, pltpu.roll(ident, ROWS, 1))

        @pl.when(s > 0)
        def _():
            result_copy(s).start()

        return carry

    lax.fori_loop(0, STEPS + 1, step, 0)

    def pair(x):
        return [x, pltpu.roll(x, 128 - ROWS, 1)]

    best = pair(outbox[0])
    for s in range(1, STEPS + 1):
        result_copy(s).wait_recv()
        best = merged(best, pair(inbox[s - 1]))
    block = slots[0]
    own = lax.dot_general(ones, jnp.concatenate([block * block] * 4, 0), NT, preferred_element_type=jnp.float32)
    dist = (best[0].astype(jnp.float32) + own[:K, :]) * (0.125 / D)
    both = jnp.concatenate([dist, best[1].astype(jnp.float32), dist, dist], 0).T
    dist_ref[...] = both[:ROWS, :K]
    near_ref[...] = both[:ROWS, K : 2 * K].astype(jnp.int32)

    for s in range(1, STEPS + 1):
        result_copy(s).wait_send()
        for chunk in range(CHUNKS):
            slot_copy(0, s, chunk, below).wait_send()
    for k in (1, 2, 3):
        id_copy(k, l).wait_send()
    for chunk in range(CAND_CHUNKS):
        for kind in range(3):
            cand_copy(l, chunk, kind, (i, l ^ 1)).wait_send()

    @pl.when(z < 4)
    def _():
        for chunk in range(CHUNKS):
            relay_copy(chunk).wait_send()


def shards(queries, candidates, cand_ids):
    dma = pltpu.SemaphoreType.DMA
    any_space = pl.BlockSpec(memory_space=pltpu.HBM)
    vmem = pl.BlockSpec(memory_space=pltpu.VMEM)
    return pl.pallas_call(
        kernel,
        out_shape=(
            jax.ShapeDtypeStruct((ROWS, K), jnp.float32),
            jax.ShapeDtypeStruct((ROWS, K), jnp.int32),
        ),
        in_specs=[any_space, any_space, any_space],
        out_specs=(vmem, vmem),
        scratch_shapes=[
            pltpu.VMEM((RELAY + 4, ROWS, D), jnp.bfloat16),
            pltpu.VMEM((LAYERS, CB, D), jnp.bfloat16),
            pltpu.VMEM((LAYERS, 1, CB), jnp.int32),
            pltpu.VMEM((CB, 128), jnp.int32),
            pltpu.VMEM((4, 8, 128), jnp.int32),
            pltpu.VMEM((K, 128), jnp.int32),
            pltpu.VMEM((K, 128), jnp.int32),
            pltpu.VMEM((STEPS + 1, K, 128), jnp.int32),
            pltpu.VMEM((STEPS, K, 128), jnp.int32),
            dma((3,)),
            dma((STEPS + 1, CHUNKS)),
            dma((RELAY + 4, CHUNKS)),
            dma((CHUNKS,)),
            dma((3, CAND_CHUNKS)),
            dma((3, CAND_CHUNKS)),
            dma((3,)),
            dma((3,)),
            dma((STEPS,)),
            dma((STEPS,)),
            pltpu.SemaphoreType.REGULAR,
        ],
        compiler_params=pltpu.CompilerParams(
            collective_id=0, has_side_effects=True, vmem_limit_bytes=16 * 1024 * 1024
        ),
    )(queries, candidates, cand_ids.reshape(1, CB))


def solution(mesh):
    return jax.shard_map(
        shards,
        mesh=mesh,
        in_specs=(P("loop", None), P(("loop", "layer"), None), P(("loop", "layer"))),
        out_specs=(P(("loop", "layer"), None), P(("loop", "layer"), None)),
        check_vma=False,
    )
```

```python
import jax
import jax.numpy as jnp
from jax import lax
from jax.experimental import pallas as pl
from jax.experimental.pallas import tpu as pltpu
from jax.sharding import PartitionSpec as P

D = 768
K = 32
STEPS = 4
LOOP = 64
ROW = 8
LAYERS = 4
CB = 128
ROWS = 32
PARKED = 5
CAND_CHUNKS = 4
CAND_PIECE = CB // CAND_CHUNKS
MESH = pl.DeviceIdType.MESH
NT = (((1,), (1,)), ((), ()))


def batcher(count):
    pairs = []
    p = 1
    while p < count:
        k = p
        while k >= 1:
            for j in range(k % p, count - k, 2 * k):
                for i in range(min(k, count - j - k)):
                    if (i + j) // (2 * p) == (i + j + k) // (2 * p):
                        pairs.append((i + j, i + j + k))
            k //= 2
        p *= 2
    return pairs


SORT16 = batcher(16)


def exchange(values, low, high):
    a, b = values[low], values[high]
    values[low], values[high] = jnp.minimum(a, b), jnp.maximum(a, b)


def settle(values):
    for gap in (8, 4, 2, 1):
        for k in range(16):
            if not k & gap:
                exchange(values, k, k + gap)


def smallest(key):
    row = lax.broadcasted_iota(jnp.int32, (8, 128), 0)
    upper = row >= 4
    v = [key[8 * g : 8 * g + 8, :] for g in range(16)]
    for low, high in SORT16:
        exchange(v, low, high)
    r = [pltpu.roll(v[15 - k], 4, 0) for k in range(16)]
    v = [jnp.where(upper, jnp.maximum(v[k], r[k]), jnp.minimum(v[k], r[k])) for k in range(16)]
    settle(v)
    for shift, lanes in ((2, 0), (3, 0), (4, 96), (4, 64)):
        r = [pltpu.roll(v[15 - k], shift, 0) for k in range(16)]
        if lanes:
            r = [pltpu.roll(x, lanes, 1) for x in r]
        v = [jnp.minimum(v[k], r[k]) for k in range(16)]
        r = [pltpu.roll(x, 4, 0) for x in v]
        v = [jnp.where(upper, jnp.maximum(v[k], r[k]), jnp.minimum(v[k], r[k])) for k in range(16)]
        settle(v)
    return v


def by_layer(parts):
    group = lax.broadcasted_iota(jnp.int32, parts[0].shape, 1) // ROWS
    return jnp.where(
        group < 2, jnp.where(group == 0, parts[0], parts[1]), jnp.where(group == 2, parts[2], parts[3])
    )


def merged(first, second):
    place = lax.broadcasted_iota(jnp.int32, (K, 128), 0)

    def before(a, b):
        return (a[0] < b[0]) | ((a[0] == b[0]) & (a[1] < b[1]))

    lower = before(first, second)
    now = [jnp.where(lower, a, b) for a, b in zip(first, second)]
    for gap in (16, 8, 4, 2, 1):
        head = (place & gap) == 0
        other = [jnp.where(head, pltpu.roll(x, K - gap, 0), pltpu.roll(x, gap, 0)) for x in now]
        keep = before(now, other) == head
        now = [jnp.where(keep, a, b) for a, b in zip(now, other)]
    return now


def kernel(
    q_ref, c_ref, id_ref, dist_ref, near_ref,
    slots, cands, idents, base, table, keys, outbox, inbox,
    local_sem, chain_send, slot_recv, park_send, spread_send, cand_send, cand_recv, id_send, id_recv,
    res_send, res_recv, ring_sem,
):
    i, l = lax.axis_index("loop"), lax.axis_index("layer")
    z = lax.rem(i, ROW)
    early = z < 4

    def at(offset):
        return (lax.rem(i + offset + 2 * LOOP, LOOP), l)

    def remote(src, dst, send, recv, device):
        return pltpu.make_async_remote_copy(
            src_ref=src, dst_ref=dst, send_sem=send, recv_sem=recv, device_id=device, device_id_type=MESH
        )

    own_q = pltpu.make_async_copy(q_ref.at[pl.ds(l * ROWS, ROWS)], slots.at[0], local_sem.at[0])
    own_c = pltpu.make_async_copy(c_ref, cands.at[l], local_sem.at[1])
    own_id = pltpu.make_async_copy(id_ref, idents.at[l], local_sem.at[2])

    barrier = pltpu.get_barrier_semaphore()

    def hello(device):
        pl.semaphore_signal(barrier, inc=1, device_id=device, device_id_type=MESH)

    @pl.when(early)
    def _():
        hello(at(ROW))

    @pl.when(z < ROW - 1)
    def _():
        hello(at(1))

    for offset in (4, 5, 6, 7):

        @pl.when(z + offset < ROW)
        def _():
            hello(at(offset))

    for k in (1, 2, 3):
        hello((i, l ^ k))
    own_q.start()
    own_id.start()
    own_c.start()
    own_q.wait()
    own_id.wait()
    pl.semaphore_wait(barrier, jnp.where(early, 4 + jnp.where(z > 0, 1, 0), z + 1))

    def park_copy():
        return remote(slots.at[0], slots.at[PARKED], park_send, slot_recv.at[PARKED], at(-ROW))

    def chain_copy(s):
        return remote(slots.at[s], slots.at[s + 1], chain_send.at[s], slot_recv.at[s + 1], at(-1))

    def spread_copy(s):
        return remote(slots.at[PARKED], slots.at[s], spread_send.at[s - 1], slot_recv.at[s], at(ROW - s))

    def arrived(slot):
        remote(slots.at[0], slots.at[slot], park_send, slot_recv.at[slot], at(1)).wait_recv()

    for e in range(4):

        @pl.when(z >= 4 + e)
        def _():
            pl.semaphore_signal(ring_sem, inc=1, device_id=at(e - z), device_id_type=MESH)

    @pl.when(early)
    def _():
        park_copy().start()

    @pl.when(z > 0)
    def _():
        chain_copy(0).start()

    def across_copy(chunk, block):
        rows = pl.ds(chunk * CAND_PIECE, CAND_PIECE)
        return remote(
            c_ref.at[rows], cands.at[block, rows], cand_send.at[0, chunk], cand_recv.at[0, chunk], (i, l ^ 2)
        )

    def beside_copy(block):
        return remote(c_ref, cands.at[block], cand_send.at[1, 0], cand_recv.at[1, 0], (i, l ^ 1))

    def onward_copy(chunk, block):
        rows = pl.ds(chunk * CAND_PIECE, CAND_PIECE)
        return remote(
            cands.at[block, rows], cands.at[block, rows],
            cand_send.at[2, chunk], cand_recv.at[2, chunk], (i, l ^ 1),
        )

    def id_copy(k, block):
        return remote(
            idents.at[block], idents.at[block], id_send.at[k - 1], id_recv.at[k - 1], (i, l ^ k)
        )

    for chunk in range(CAND_CHUNKS):
        across_copy(chunk, l).start()
    for k in (1, 2, 3):
        id_copy(k, l).start()
    beside_copy(l).start()

    for k in (1, 2, 3):
        id_copy(k, l ^ k).wait_recv()
    lane = lax.broadcasted_iota(jnp.int32, (CB, 128), 1)
    id_rows = [idents[m].astype(jnp.float32) for m in range(LAYERS)]
    id_cols = jnp.concatenate([jnp.broadcast_to(x, (ROWS, CB)) for x in id_rows], 0).T
    part = jnp.zeros((CB, 128), jnp.float32)
    for m in range(LAYERS):
        for k in range(4):
            shifted = pltpu.roll(jnp.broadcast_to(id_rows[m], (8, 128)), 32 * k, 1)[:1]
            part += jnp.where(shifted < id_cols, 1.0, 0.0)
    same = lax.broadcasted_iota(jnp.int32, (128, 128), 0) // ROWS == (
        lax.broadcasted_iota(jnp.int32, (128, 128), 1) // ROWS
    )
    rank = jnp.dot(
        part.astype(jnp.bfloat16),
        jnp.where(same, 1.0, 0.0).astype(jnp.bfloat16),
        preferred_element_type=jnp.float32,
    ).astype(jnp.int32)
    for a in range(4):
        total = jnp.zeros((1, 128), jnp.float32)
        for m in range(LAYERS):
            column = rank[:, ROWS * m : ROWS * m + 1]
            ident = id_cols[:, ROWS * m : ROWS * m + 1]
            total += jnp.sum(jnp.where(column == lane + 128 * a, ident, 0.0), 0, keepdims=True)
        table[a] = jnp.broadcast_to(total, (8, 128)).astype(jnp.int32)

    @pl.when((z > 0) & (z < ROW - 1))
    def _():
        arrived(1)
        chain_copy(1).start()

    @pl.when(early)
    def _():
        arrived(PARKED)
        pl.semaphore_wait(ring_sem, 4 - z)
        for s in (4, 3, 2, 1):

            @pl.when(s > z)
            def _():
                spread_copy(s).start()

    for chunk in range(CAND_CHUNKS):
        across_copy(chunk, l ^ 2).wait_recv()
        onward_copy(chunk, l ^ 2).start()
    own_c.wait()
    beside_copy(l ^ 1).wait_recv()
    for chunk in range(CAND_CHUNKS):
        onward_copy(chunk, l ^ 3).wait_recv()

    ones = jnp.ones((128, D), jnp.bfloat16)
    norms = []
    for m in range(LAYERS):
        block = cands[m]
        norms.append(lax.dot_general(block * block, ones, NT, preferred_element_type=jnp.float32))
    base[...] = by_layer(norms).astype(jnp.int32) * 512 + rank

    def result_copy(s):
        return remote(
            outbox.at[s], inbox.at[s - 1], res_send.at[s - 1], res_recv.at[s - 1], at(s)
        )

    def step(t, carry):
        s = jnp.where(
            (z == 4) & (t >= 2),
            jnp.where(t == 2, 4, t - 1),
            jnp.where((z == 5) & ((t == 2) | (t == 3)), 5 - t, t),
        )

        @pl.when((s >= 2) | ((s == 1) & ((z == 0) | (z == ROW - 1))))
        def _():
            arrived(s)

        @pl.when((z > 0) & (s >= 2) & (s <= 3) & (s + z < ROW))
        def _():
            chain_copy(s).start()

        block = slots[s]
        four = jnp.concatenate([block] * 4, 0)
        inner = by_layer(
            [lax.dot_general(cands[m], four, NT, preferred_element_type=jnp.float32) for m in range(LAYERS)]
        )
        v = smallest(base[...] - inner.astype(jnp.int32) * 1024)

        @pl.when(s == 0)
        def _():
            for k in range(16):
                keys[k : k + 1, :] = v[k][0:1, :]
                keys[16 + k : 17 + k, :] = v[k][4:5, :]

        @pl.when(s > 0)
        def _():
            for k in range(16):
                keys[31 - k : 32 - k, :] = v[k][0:1, :]
                keys[15 - k : 16 - k, :] = v[k][4:5, :]

        left = lax.broadcasted_iota(jnp.int32, (8, 128), 1) < ROWS
        for g in range(4):
            key = keys[8 * g : 8 * g + 8, :]
            place = key & 127
            which = (key >> 7) & 3
            found = [jnp.take_along_axis(table[a], place, axis=1, mode="promise_in_bounds") for a in range(4)]
            ident = jnp.where(
                which < 2, jnp.where(which == 0, found[0], found[1]), jnp.where(which == 2, found[2], found[3])
            )
            outbox[s, 8 * g : 8 * g + 8, :] = jnp.where(left, key >> 9, pltpu.roll(ident, ROWS, 1))

        @pl.when(s > 0)
        def _():
            result_copy(s).start()

        return carry

    lax.fori_loop(0, STEPS + 1, step, 0)

    def pair(x):
        return [x, pltpu.roll(x, 128 - ROWS, 1)]

    best = pair(outbox[0])
    for s in range(1, STEPS + 1):
        result_copy(s).wait_recv()
        best = merged(best, pair(inbox[s - 1]))
    block = slots[0]
    own = lax.dot_general(ones, jnp.concatenate([block * block] * 4, 0), NT, preferred_element_type=jnp.float32)
    dist = (best[0].astype(jnp.float32) + own[:K, :]) * (0.125 / D)
    both = jnp.concatenate([dist, best[1].astype(jnp.float32), dist, dist], 0).T
    dist_ref[...] = both[:ROWS, :K]
    near_ref[...] = both[:ROWS, K : 2 * K].astype(jnp.int32)

    for s in range(1, STEPS + 1):
        result_copy(s).wait_send()

        @pl.when((z > 0) & (s - 1 + z < ROW))
        def _():
            chain_copy(s - 1).wait_send()

        @pl.when(early & (s > z))
        def _():
            spread_copy(s).wait_send()

    for k in (1, 2, 3):
        id_copy(k, l).wait_send()
    beside_copy(l).wait_send()
    for chunk in range(CAND_CHUNKS):
        across_copy(chunk, l).wait_send()
        onward_copy(chunk, l).wait_send()

    @pl.when(early)
    def _():
        park_copy().wait_send()


def shards(queries, candidates, cand_ids):
    dma = pltpu.SemaphoreType.DMA
    any_space = pl.BlockSpec(memory_space=pltpu.HBM)
    vmem = pl.BlockSpec(memory_space=pltpu.VMEM)
    return pl.pallas_call(
        kernel,
        out_shape=(
            jax.ShapeDtypeStruct((ROWS, K), jnp.float32),
            jax.ShapeDtypeStruct((ROWS, K), jnp.int32),
        ),
        in_specs=[any_space, any_space, any_space],
        out_specs=(vmem, vmem),
        scratch_shapes=[
            pltpu.VMEM((PARKED + 1, ROWS, D), jnp.bfloat16),
            pltpu.VMEM((LAYERS, CB, D), jnp.bfloat16),
            pltpu.VMEM((LAYERS, 1, CB), jnp.int32),
            pltpu.VMEM((CB, 128), jnp.int32),
            pltpu.VMEM((4, 8, 128), jnp.int32),
            pltpu.VMEM((K, 128), jnp.int32),
            pltpu.VMEM((STEPS + 1, K, 128), jnp.int32),
            pltpu.VMEM((STEPS, K, 128), jnp.int32),
            dma((3,)),
            dma((STEPS,)),
            dma((PARKED + 1,)),
            dma,
            dma((STEPS,)),
            dma((3, CAND_CHUNKS)),
            dma((3, CAND_CHUNKS)),
            dma((3,)),
            dma((3,)),
            dma((STEPS,)),
            dma((STEPS,)),
            pltpu.SemaphoreType.REGULAR,
        ],
        compiler_params=pltpu.CompilerParams(
            collective_id=0, has_side_effects=True, vmem_limit_bytes=16 * 1024 * 1024
        ),
    )(*(pltpu.with_memory_space_constraint(x, pltpu.HBM) for x in (queries, candidates, cand_ids.reshape(1, CB))))


def solution(mesh):
    return jax.shard_map(
        shards,
        mesh=mesh,
        in_specs=(P("loop", None), P(("loop", "layer"), None), P(("loop", "layer"))),
        out_specs=(P(("loop", "layer"), None), P(("loop", "layer"), None)),
        check_vma=False,
    )
```

```python
import jax
import jax.numpy as jnp
from jax import lax
from jax.experimental import pallas as pl
from jax.experimental.pallas import tpu as pltpu
from jax.sharding import PartitionSpec as P

D = 768
K = 32
STEPS = 4
LOOP = 64
ROW = 8
LAYERS = 4
CB = 128
ROWS = 32
PARKED = 5
CAND_CHUNKS = 8
CAND_PIECE = CB // CAND_CHUNKS
MESH = pl.DeviceIdType.MESH
NT = (((1,), (1,)), ((), ()))


def batcher(count):
    pairs = []
    p = 1
    while p < count:
        k = p
        while k >= 1:
            for j in range(k % p, count - k, 2 * k):
                for i in range(min(k, count - j - k)):
                    if (i + j) // (2 * p) == (i + j + k) // (2 * p):
                        pairs.append((i + j, i + j + k))
            k //= 2
        p *= 2
    return pairs


SORT16 = batcher(16)


def exchange(values, low, high):
    a, b = values[low], values[high]
    values[low], values[high] = jnp.minimum(a, b), jnp.maximum(a, b)


def settle(values):
    for gap in (8, 4, 2, 1):
        for k in range(16):
            if not k & gap:
                exchange(values, k, k + gap)


def smallest(key):
    row = lax.broadcasted_iota(jnp.int32, (8, 128), 0)
    upper = row >= 4
    v = [key[8 * g : 8 * g + 8, :] for g in range(16)]
    for low, high in SORT16:
        exchange(v, low, high)
    r = [pltpu.roll(v[15 - k], 4, 0) for k in range(16)]
    v = [jnp.where(upper, jnp.maximum(v[k], r[k]), jnp.minimum(v[k], r[k])) for k in range(16)]
    settle(v)
    for shift, lanes in ((2, 0), (3, 0), (4, 96), (4, 64)):
        r = [pltpu.roll(v[15 - k], shift, 0) for k in range(16)]
        if lanes:
            r = [pltpu.roll(x, lanes, 1) for x in r]
        v = [jnp.minimum(v[k], r[k]) for k in range(16)]
        r = [pltpu.roll(x, 4, 0) for x in v]
        v = [jnp.where(upper, jnp.maximum(v[k], r[k]), jnp.minimum(v[k], r[k])) for k in range(16)]
        settle(v)
    return v


def by_layer(parts):
    group = lax.broadcasted_iota(jnp.int32, parts[0].shape, 1) // ROWS
    return jnp.where(
        group < 2, jnp.where(group == 0, parts[0], parts[1]), jnp.where(group == 2, parts[2], parts[3])
    )


def merged(first, second):
    place = lax.broadcasted_iota(jnp.int32, (K, 128), 0)

    def before(a, b):
        return (a[0] < b[0]) | ((a[0] == b[0]) & (a[1] < b[1]))

    lower = before(first, second)
    now = [jnp.where(lower, a, b) for a, b in zip(first, second)]
    for gap in (16, 8, 4, 2, 1):
        head = (place & gap) == 0
        other = [jnp.where(head, pltpu.roll(x, K - gap, 0), pltpu.roll(x, gap, 0)) for x in now]
        keep = before(now, other) == head
        now = [jnp.where(keep, a, b) for a, b in zip(now, other)]
    return now


def kernel(
    q_ref, c_ref, id_ref, dist_ref, near_ref,
    slots, cands, idents, base, table, keys, outbox, inbox,
    local_sem, chain_send, slot_recv, park_send, spread_send, cand_send, cand_recv, id_send, id_recv,
    res_send, res_recv, ring_sem, go_sem,
):
    i, l = lax.axis_index("loop"), lax.axis_index("layer")
    z = lax.rem(i, ROW)
    early = z < 4
    skew = (z == 1) | (z == 2)

    def at(offset, layer=l):
        return (lax.rem(i + offset + 2 * LOOP, LOOP), layer)

    over = l ^ 2

    def remote(src, dst, send, recv, device):
        return pltpu.make_async_remote_copy(
            src_ref=src, dst_ref=dst, send_sem=send, recv_sem=recv, device_id=device, device_id_type=MESH
        )

    own_rows = q_ref.at[pl.ds(l * ROWS, ROWS)]
    own_q = pltpu.make_async_copy(own_rows, slots.at[0], local_sem.at[0])
    own_c = pltpu.make_async_copy(c_ref, cands.at[l], local_sem.at[1])
    own_id = pltpu.make_async_copy(id_ref, idents.at[l], local_sem.at[2])

    barrier = pltpu.get_barrier_semaphore()

    def hello(device):
        pl.semaphore_signal(barrier, inc=1, device_id=device, device_id_type=MESH)

    def when_z(*places):
        hit = z == places[0]
        for place in places[1:]:
            hit = hit | (z == place)
        return pl.when(hit)

    @when_z(0, 3)
    def _():
        hello(at(ROW, over))

    @when_z(2, 3)
    def _():
        hello(at(ROW - 1, over))

    @pl.when(z < ROW - 1)
    def _():
        hello(at(1))

    for place, late in ((0, (4, 5, 6, 7)), (2, (5, 6, 7)), (3, (6, 7))):

        @when_z(place)
        def _():
            for other in late:
                hello(at(other - place))

    for k in (1, 2, 3):
        hello((i, l ^ k))
    own_q.start()
    own_id.start()
    own_c.start()
    expected = jnp.where(z == 0, 4, jnp.where(z <= 4, 5, jnp.where(z == 5, 6, 7)))
    pl.semaphore_wait(barrier, expected)

    def park_copy():
        slot = jnp.where(z == 2, PARKED + 1, PARKED)
        device = at(jnp.where(skew, 1 - ROW, -ROW), over)
        return remote(own_rows, slots.at[slot], park_send, slot_recv.at[slot], device)

    def first_copy():
        return remote(own_rows, slots.at[1], chain_send.at[0], slot_recv.at[1], at(-1))

    def chain_copy(s):
        return remote(slots.at[s], slots.at[s + 1], chain_send.at[s], slot_recv.at[s + 1], at(-1))

    def spread_copy(n, source, offset, slot):
        return remote(slots.at[source], slots.at[slot], spread_send.at[n], slot_recv.at[slot], at(offset))

    def arrived(slot):
        remote(slots.at[0], slots.at[slot], park_send, slot_recv.at[slot], at(1)).wait_recv()

    for late, places in ((4, (0,)), (5, (0, 2)), (6, (0, 2, 3)), (7, (0, 2, 3))):

        @when_z(late)
        def _():
            for place in places:
                pl.semaphore_signal(
                    ring_sem.at[late - 4], inc=1, device_id=at(place - late), device_id_type=MESH
                )

    @pl.when(early)
    def _():
        park_copy().start()

    @pl.when(z > 0)
    def _():
        first_copy().start()

    def across_copy(chunk, block):
        rows = pl.ds(chunk * CAND_PIECE, CAND_PIECE)
        return remote(
            c_ref.at[rows], cands.at[block, rows], cand_send.at[0, chunk], cand_recv.at[0, chunk], (i, l ^ 2)
        )

    def beside_copy(block):
        return remote(c_ref, cands.at[block], cand_send.at[1, 0], cand_recv.at[1, 0], (i, l ^ 1))

    def onward_copy(chunk, block):
        rows = pl.ds(chunk * CAND_PIECE, CAND_PIECE)
        return remote(
            cands.at[block, rows], cands.at[block, rows],
            cand_send.at[2, chunk], cand_recv.at[2, chunk], (i, l ^ 1),
        )

    def id_copy(k, block):
        return remote(id_ref, idents.at[block], id_send.at[k - 1], id_recv.at[k - 1], (i, l ^ k))

    for k in (1, 2, 3):
        id_copy(k, l).start()
    for chunk in range(CAND_CHUNKS):
        across_copy(chunk, l).start()
    beside_copy(l).start()

    @pl.when((z > 0) & (z < ROW - 1))
    def _():
        arrived(1)
        chain_copy(1).start()

    @when_z(0)
    def _():
        arrived(PARKED)
        for n, late in enumerate((7, 6, 4, 5)):
            pl.semaphore_wait(ring_sem.at[late - 4], 1)
            spread_copy(n, PARKED, late, 8 - late).start()

    own_id.wait()
    for k in (1, 2, 3):
        id_copy(k, l ^ k).wait_recv()
    lane = lax.broadcasted_iota(jnp.int32, (CB, 128), 1)
    id_rows = [idents[m].astype(jnp.float32) for m in range(LAYERS)]
    id_cols = jnp.concatenate([jnp.broadcast_to(x, (ROWS, CB)) for x in id_rows], 0).T
    part = jnp.zeros((CB, 128), jnp.float32)
    for m in range(LAYERS):
        for k in range(4):
            shifted = pltpu.roll(jnp.broadcast_to(id_rows[m], (8, 128)), 32 * k, 1)[:1]
            part += jnp.where(shifted < id_cols, 1.0, 0.0)
    same = lax.broadcasted_iota(jnp.int32, (128, 128), 0) // ROWS == (
        lax.broadcasted_iota(jnp.int32, (128, 128), 1) // ROWS
    )
    rank = jnp.dot(
        part.astype(jnp.bfloat16),
        jnp.where(same, 1.0, 0.0).astype(jnp.bfloat16),
        preferred_element_type=jnp.float32,
    ).astype(jnp.int32)
    for a in range(4):
        total = jnp.zeros((1, 128), jnp.float32)
        for m in range(LAYERS):
            column = rank[:, ROWS * m : ROWS * m + 1]
            ident = id_cols[:, ROWS * m : ROWS * m + 1]
            total += jnp.sum(jnp.where(column == lane + 128 * a, ident, 0.0), 0, keepdims=True)
        table[a] = jnp.broadcast_to(total, (8, 128)).astype(jnp.int32)

    for chunk in range(CAND_CHUNKS):
        across_copy(chunk, l ^ 2).wait_recv()
        onward_copy(chunk, l ^ 2).start()

    @when_z(0)
    def _():
        arrived(2)
        for n in range(3):
            spread_copy(n, PARKED, 4, 4).wait_send()
        pl.semaphore_signal(go_sem, inc=1, device_id=at(2), device_id_type=MESH)

    @when_z(2)
    def _():
        for late in (5, 6, 7):
            pl.semaphore_wait(ring_sem.at[late - 4], 1)
        arrived(PARKED)
        spread_copy(0, PARKED, 3, 4).start()

    @when_z(3)
    def _():
        for late in (6, 7):
            pl.semaphore_wait(ring_sem.at[late - 4], 1)
        arrived(PARKED + 1)
        spread_copy(0, PARKED + 1, 3, 4).start()

    @pl.when((z > 0) & (z < ROW - 2))
    def _():
        arrived(2)
        chain_copy(2).start()

    @when_z(2)
    def _():
        pl.semaphore_wait(go_sem, 1)
        spread_copy(1, PARKED, 4, 3).start()
        spread_copy(2, PARKED, 5, 2).start()
        spread_copy(1, PARKED, 4, 3).wait_send()
        pl.semaphore_signal(go_sem, inc=1, device_id=at(1), device_id_type=MESH)

    @when_z(3)
    def _():
        pl.semaphore_wait(go_sem, 1)
        spread_copy(1, PARKED + 1, 4, 3).start()
        arrived(PARKED)
        spread_copy(2, PARKED, 4, 4).start()

    own_q.wait()
    own_c.wait()
    beside_copy(l ^ 1).wait_recv()
    for chunk in range(CAND_CHUNKS):
        onward_copy(chunk, l ^ 3).wait_recv()

    ones = jnp.ones((128, D), jnp.bfloat16)
    norms = []
    for m in range(LAYERS):
        block = cands[m]
        norms.append(lax.dot_general(block * block, ones, NT, preferred_element_type=jnp.float32))
    base[...] = by_layer(norms).astype(jnp.int32) * 512 + rank

    def result_copy(s):
        return remote(
            outbox.at[s], inbox.at[s - 1], res_send.at[s - 1], res_recv.at[s - 1],
            at(s, jnp.where(z + s >= ROW, over, l)),
        )

    def step(t, carry):
        s = jnp.where(z == 4, lax.rem(t + 4, 5), jnp.where(z == 5, lax.rem(t + 3, 5), t))
        s = jnp.where(z == 6, jnp.where(t == 0, 2, jnp.where(t < 3, t - 1, 7 - t)), s)
        s = jnp.where((z == 7) & (t < 2), 1 - t, s)

        chained = (z > 0) & (z < 5)

        @pl.when(chained & (t == jnp.where(z == 4, 2, 1)))
        def _():
            arrived(3)
            chain_copy(3).start()

        late_slot = ((s == 3) & ~chained) | (s == 4)

        @pl.when(late_slot | ((s == 2) & (z >= 6)) | ((s == 1) & ((z == 0) | (z == ROW - 1))))
        def _():
            arrived(s)

        block = slots[s]
        four = jnp.concatenate([block] * 4, 0)
        inner = by_layer(
            [lax.dot_general(cands[m], four, NT, preferred_element_type=jnp.float32) for m in range(LAYERS)]
        )
        v = smallest(base[...] - inner.astype(jnp.int32) * 1024)

        @pl.when(s == 0)
        def _():
            for k in range(16):
                keys[k : k + 1, :] = v[k][0:1, :]
                keys[16 + k : 17 + k, :] = v[k][4:5, :]

        @pl.when(s > 0)
        def _():
            for k in range(16):
                keys[31 - k : 32 - k, :] = v[k][0:1, :]
                keys[15 - k : 16 - k, :] = v[k][4:5, :]

        lanes = lax.broadcasted_iota(jnp.int32, (8, 128), 1)
        both = []
        for g in range(4):
            key = keys[8 * g : 8 * g + 8, :]
            place = key & 127
            which = (key >> 7) & 3
            found = [jnp.take_along_axis(table[a], place, axis=1, mode="promise_in_bounds") for a in range(4)]
            ident = jnp.where(
                which < 2, jnp.where(which == 0, found[0], found[1]), jnp.where(which == 2, found[2], found[3])
            )
            both.append(jnp.where(lanes < ROWS, key >> 9, pltpu.roll(ident, ROWS, 1)))
        for g in range(2):
            outbox[s, 8 * g : 8 * g + 8, :] = jnp.where(lanes < 64, both[g], pltpu.roll(both[g + 2], 64, 1))

        @pl.when(s > 0)
        def _():
            result_copy(s).start()

        return carry

    lax.fori_loop(0, STEPS + 1, step, 0)

    def pair(x):
        whole = jnp.concatenate([x, pltpu.roll(x, 64, 1)], 0)
        return [whole, pltpu.roll(whole, 128 - ROWS, 1)]

    best = pair(outbox[0])
    for s in range(1, STEPS + 1):
        result_copy(s).wait_recv()
        best = merged(best, pair(inbox[s - 1]))
    block = slots[0]
    own = lax.dot_general(ones, jnp.concatenate([block * block] * 4, 0), NT, preferred_element_type=jnp.float32)
    dist = (best[0].astype(jnp.float32) + own[:K, :]) * (0.125 / D)
    both = jnp.concatenate([dist, best[1].astype(jnp.float32), dist, dist], 0).T
    dist_ref[...] = both[:ROWS, :K]
    near_ref[...] = both[:ROWS, K : 2 * K].astype(jnp.int32)

    for s in range(1, STEPS + 1):
        result_copy(s).wait_send()

        @pl.when((z > 0) & (s - 1 + z < ROW))
        def _():
            chain_copy(s - 1).wait_send()

    for n, places in enumerate(((2, 3), (3,), (2, 3), (0,))):

        @when_z(*places)
        def _():
            spread_copy(n, PARKED, 4, 4).wait_send()

    for k in (1, 2, 3):
        id_copy(k, l).wait_send()
    beside_copy(l).wait_send()
    for chunk in range(CAND_CHUNKS):
        across_copy(chunk, l).wait_send()
        onward_copy(chunk, l).wait_send()

    @pl.when(early)
    def _():
        park_copy().wait_send()


def shards(queries, candidates, cand_ids):
    dma = pltpu.SemaphoreType.DMA
    any_space = pl.BlockSpec(memory_space=pltpu.HBM)
    vmem = pl.BlockSpec(memory_space=pltpu.VMEM)
    return pl.pallas_call(
        kernel,
        out_shape=(
            jax.ShapeDtypeStruct((ROWS, K), jnp.float32),
            jax.ShapeDtypeStruct((ROWS, K), jnp.int32),
        ),
        in_specs=[any_space, any_space, any_space],
        out_specs=(vmem, vmem),
        scratch_shapes=[
            pltpu.VMEM((PARKED + 2, ROWS, D), jnp.bfloat16),
            pltpu.VMEM((LAYERS, CB, D), jnp.bfloat16),
            pltpu.VMEM((LAYERS, 1, CB), jnp.int32),
            pltpu.VMEM((CB, 128), jnp.int32),
            pltpu.VMEM((4, 8, 128), jnp.int32),
            pltpu.VMEM((K, 128), jnp.int32),
            pltpu.VMEM((STEPS + 1, K // 2, 128), jnp.int32),
            pltpu.VMEM((STEPS, K // 2, 128), jnp.int32),
            dma((3,)),
            dma((STEPS,)),
            dma((PARKED + 2,)),
            dma,
            dma((STEPS,)),
            dma((3, CAND_CHUNKS)),
            dma((3, CAND_CHUNKS)),
            dma((3,)),
            dma((3,)),
            dma((STEPS,)),
            dma((STEPS,)),
            pltpu.SemaphoreType.REGULAR((4,)),
            pltpu.SemaphoreType.REGULAR,
        ],
        compiler_params=pltpu.CompilerParams(
            collective_id=0, has_side_effects=True, vmem_limit_bytes=16 * 1024 * 1024
        ),
    )(*(pltpu.with_memory_space_constraint(x, pltpu.HBM) for x in (queries, candidates, cand_ids.reshape(1, CB))))


def solution(mesh):
    return jax.shard_map(
        shards,
        mesh=mesh,
        in_specs=(P("loop", None), P(("loop", "layer"), None), P(("loop", "layer"))),
        out_specs=(P(("loop", "layer"), None), P(("loop", "layer"), None)),
        check_vma=False,
    )
```

```python
import jax
import jax.numpy as jnp
from jax import lax
from jax.experimental import pallas as pl
from jax.experimental.pallas import tpu as pltpu
from jax.sharding import PartitionSpec as P

D = 768
K = 32
STEPS = 4
LOOP = 64
ROW = 8
LAYERS = 4
CB = 128
ROWS = 32
PARKED = 5
CAND_CHUNKS = 8
CAND_PIECE = CB // CAND_CHUNKS
MESH = pl.DeviceIdType.MESH
NT = (((1,), (1,)), ((), ()))


def batcher(count):
    pairs = []
    p = 1
    while p < count:
        k = p
        while k >= 1:
            for j in range(k % p, count - k, 2 * k):
                for i in range(min(k, count - j - k)):
                    if (i + j) // (2 * p) == (i + j + k) // (2 * p):
                        pairs.append((i + j, i + j + k))
            k //= 2
        p *= 2
    return pairs


SORT16 = batcher(16)


def exchange(values, low, high):
    a, b = values[low], values[high]
    values[low], values[high] = jnp.minimum(a, b), jnp.maximum(a, b)


def settle(values):
    for gap in (8, 4, 2, 1):
        for k in range(16):
            if not k & gap:
                exchange(values, k, k + gap)


def smallest(key):
    row = lax.broadcasted_iota(jnp.int32, (8, 128), 0)
    upper = row >= 4
    v = [key[8 * g : 8 * g + 8, :] for g in range(16)]
    for low, high in SORT16:
        exchange(v, low, high)
    r = [pltpu.roll(v[15 - k], 4, 0) for k in range(16)]
    v = [jnp.where(upper, jnp.maximum(v[k], r[k]), jnp.minimum(v[k], r[k])) for k in range(16)]
    settle(v)
    for shift, lanes in ((2, 0), (3, 0), (4, 96), (4, 64)):
        r = [pltpu.roll(v[15 - k], shift, 0) for k in range(16)]
        if lanes:
            r = [pltpu.roll(x, lanes, 1) for x in r]
        v = [jnp.minimum(v[k], r[k]) for k in range(16)]
        r = [pltpu.roll(x, 4, 0) for x in v]
        v = [jnp.where(upper, jnp.maximum(v[k], r[k]), jnp.minimum(v[k], r[k])) for k in range(16)]
        settle(v)
    return v


def by_layer(parts):
    group = lax.broadcasted_iota(jnp.int32, parts[0].shape, 1) // ROWS
    return jnp.where(
        group < 2, jnp.where(group == 0, parts[0], parts[1]), jnp.where(group == 2, parts[2], parts[3])
    )


def merged(first, second):
    place = lax.broadcasted_iota(jnp.int32, (K, 128), 0)

    def before(a, b):
        return (a[0] < b[0]) | ((a[0] == b[0]) & (a[1] < b[1]))

    lower = before(first, second)
    now = [jnp.where(lower, a, b) for a, b in zip(first, second)]
    for gap in (16, 8, 4, 2, 1):
        head = (place & gap) == 0
        other = [jnp.where(head, pltpu.roll(x, K - gap, 0), pltpu.roll(x, gap, 0)) for x in now]
        keep = before(now, other) == head
        now = [jnp.where(keep, a, b) for a, b in zip(now, other)]
    return now


def kernel(
    q_ref, c_ref, id_ref, out_ref,
    slots, cands, idents, base, table, keys, outbox, inbox,
    local_sem, chain_send, slot_recv, park_send, spread_send, cand_send, cand_recv, id_send, id_recv,
    res_send, res_recv, ring_sem,
):
    i, l = lax.axis_index("loop"), lax.axis_index("layer")
    z = lax.rem(i, ROW)
    early = z < 4
    skew = (z == 1) | (z == 2)

    def at(offset, layer=l):
        return (lax.rem(i + offset + 2 * LOOP, LOOP), layer)

    over = l ^ 2
    keeper = (l & 1) == 1
    lower = l & 2

    def remote(src, dst, send, recv, device):
        return pltpu.make_async_remote_copy(
            src_ref=src, dst_ref=dst, send_sem=send, recv_sem=recv, device_id=device, device_id_type=MESH
        )

    own_rows = q_ref.at[pl.ds(l * ROWS, ROWS)]
    own_q = pltpu.make_async_copy(own_rows, slots.at[0], local_sem.at[0])
    own_c = pltpu.make_async_copy(c_ref, cands.at[l], local_sem.at[1])
    own_id = pltpu.make_async_copy(id_ref, idents.at[l], local_sem.at[2])

    barrier = pltpu.get_barrier_semaphore()

    def hello(device):
        pl.semaphore_signal(barrier, inc=1, device_id=device, device_id_type=MESH)

    def when_z(*places):
        hit = z == places[0]
        for place in places[1:]:
            hit = hit | (z == place)
        return pl.when(hit)

    def when_keeper(*places):
        hit = z == places[0]
        for place in places[1:]:
            hit = hit | (z == place)
        return pl.when(hit & keeper)

    @when_keeper(0, 3)
    def _():
        hello(at(ROW, over))
        hello(at(ROW, over ^ 1))

    @when_keeper(2, 3)
    def _():
        hello(at(ROW - 1, over))
        hello(at(ROW - 1, over ^ 1))

    @pl.when(z < ROW - 1)
    def _():
        hello(at(1))

    for place, late in ((0, (4, 5, 6, 7)), (2, (5, 6, 7)), (3, (6, 7))):

        @when_keeper(place)
        def _():
            for other in late:
                hello(at(other - place))
                hello(at(other - place, lower))

    for k in (1, 2, 3):
        hello((i, l ^ k))
    own_q.start()
    own_id.start()
    own_c.start()
    expected = jnp.where(z == 0, 4, jnp.where(z <= 4, 5, jnp.where(z == 5, 6, 7)))
    pl.semaphore_wait(barrier, expected)

    def park_copy():
        slot = jnp.where(z == 2, PARKED + 1, PARKED) + jnp.where(keeper, 0, 2)
        device = at(jnp.where(skew, 1 - ROW, -ROW), over | 1)
        return remote(slots.at[0], slots.at[slot], park_send, slot_recv.at[slot], device)

    def first_copy():
        return remote(own_rows, slots.at[1], chain_send.at[0], slot_recv.at[1], at(-1))

    def chain_copy(s):
        return remote(slots.at[s], slots.at[s + 1], chain_send.at[s], slot_recv.at[s + 1], at(-1))

    def spread_copy(n, source, offset, slot):
        return remote(slots.at[source], slots.at[slot], spread_send.at[n], slot_recv.at[slot], at(offset))

    def lower_copy(n, source, offset, slot):
        return remote(
            slots.at[source + 2], slots.at[slot], spread_send.at[n + 4], slot_recv.at[slot], at(offset, lower)
        )

    def arrived(slot):
        remote(slots.at[0], slots.at[slot], park_send, slot_recv.at[slot], at(1)).wait_recv()

    for late, places in ((4, (0,)), (5, (0, 2)), (6, (0, 2, 3)), (7, (0, 2, 3))):

        @when_z(late)
        def _():
            for place in places:
                pl.semaphore_signal(
                    ring_sem.at[late - 4], inc=1, device_id=at(place - late, l | 1), device_id_type=MESH
                )

    own_q.wait()

    @pl.when(early)
    def _():
        park_copy().start()

    @pl.when(z > 0)
    def _():
        first_copy().start()

    def across_copy(chunk, block):
        rows = pl.ds(chunk * CAND_PIECE, CAND_PIECE)
        return remote(
            c_ref.at[rows], cands.at[block, rows], cand_send.at[0, chunk], cand_recv.at[0, chunk], (i, l ^ 2)
        )

    def beside_copy(block):
        return remote(c_ref, cands.at[block], cand_send.at[1, 0], cand_recv.at[1, 0], (i, l ^ 1))

    def onward_copy(chunk, block):
        rows = pl.ds(chunk * CAND_PIECE, CAND_PIECE)
        return remote(
            cands.at[block, rows], cands.at[block, rows],
            cand_send.at[2, chunk], cand_recv.at[2, chunk], (i, l ^ 1),
        )

    def id_copy(k, block):
        return remote(id_ref, idents.at[block], id_send.at[k - 1], id_recv.at[k - 1], (i, l ^ k))

    for k in (1, 2, 3):
        id_copy(k, l).start()
    for chunk in range(CAND_CHUNKS):
        across_copy(chunk, l).start()
    beside_copy(l).start()

    @pl.when((z > 0) & (z < ROW - 1))
    def _():
        arrived(1)
        chain_copy(1).start()

    @when_keeper(0)
    def _():
        arrived(PARKED)
        for n, late in enumerate((7, 6, 4, 5)):
            pl.semaphore_wait(ring_sem.at[late - 4], 2)
            spread_copy(n, PARKED, late, 8 - late).start()
        arrived(PARKED + 2)
        for n, late in enumerate((7, 6, 4, 5)):
            lower_copy(n, PARKED, late, 8 - late).start()

    own_id.wait()
    for k in (1, 2, 3):
        id_copy(k, l ^ k).wait_recv()
    lane = lax.broadcasted_iota(jnp.int32, (CB, 128), 1)
    id_rows = [idents[m].astype(jnp.float32) for m in range(LAYERS)]
    id_cols = jnp.concatenate([jnp.broadcast_to(x, (ROWS, CB)) for x in id_rows], 0).T
    part = jnp.zeros((CB, 128), jnp.float32)
    for m in range(LAYERS):
        for k in range(4):
            shifted = pltpu.roll(jnp.broadcast_to(id_rows[m], (8, 128)), 32 * k, 1)[:1]
            part += jnp.where(shifted < id_cols, 1.0, 0.0)
    same = lax.broadcasted_iota(jnp.int32, (128, 128), 0) // ROWS == (
        lax.broadcasted_iota(jnp.int32, (128, 128), 1) // ROWS
    )
    rank = jnp.dot(
        part.astype(jnp.bfloat16),
        jnp.where(same, 1.0, 0.0).astype(jnp.bfloat16),
        preferred_element_type=jnp.float32,
    ).astype(jnp.int32)
    for a in range(4):
        total = jnp.zeros((1, 128), jnp.float32)
        for m in range(LAYERS):
            column = rank[:, ROWS * m : ROWS * m + 1]
            ident = id_cols[:, ROWS * m : ROWS * m + 1]
            total += jnp.sum(jnp.where(column == lane + 128 * a, ident, 0.0), 0, keepdims=True)
        table[a] = jnp.broadcast_to(total, (8, 128)).astype(jnp.int32)

    for chunk in range(CAND_CHUNKS):
        across_copy(chunk, l ^ 2).wait_recv()
        onward_copy(chunk, l ^ 2).start()

    @when_keeper(2)
    def _():
        for late in (5, 6, 7):
            pl.semaphore_wait(ring_sem.at[late - 4], 2)
        arrived(PARKED)
        for n, (offset, slot) in enumerate(((3, 4), (4, 3), (5, 2))):
            spread_copy(n, PARKED, offset, slot).start()
        arrived(PARKED + 2)
        for n, (offset, slot) in enumerate(((3, 4), (4, 3), (5, 2))):
            lower_copy(n, PARKED, offset, slot).start()

    @when_keeper(3)
    def _():
        for late in (6, 7):
            pl.semaphore_wait(ring_sem.at[late - 4], 2)
        for copy, extra in ((spread_copy, 0), (lower_copy, 2)):
            arrived(PARKED + extra)
            copy(0, PARKED, 4, 4).start()
            arrived(PARKED + 1 + extra)
            copy(1, PARKED + 1, 3, 4).start()
            copy(2, PARKED + 1, 4, 3).start()

    @pl.when((z > 0) & (z < ROW - 2))
    def _():
        arrived(2)
        chain_copy(2).start()

    own_c.wait()
    beside_copy(l ^ 1).wait_recv()
    for chunk in range(CAND_CHUNKS):
        onward_copy(chunk, l ^ 3).wait_recv()

    ones = jnp.ones((128, D), jnp.bfloat16)
    norms = []
    for m in range(LAYERS):
        block = cands[m]
        norms.append(lax.dot_general(block * block, ones, NT, preferred_element_type=jnp.float32))
    base[...] = by_layer(norms).astype(jnp.int32) * 512 + rank

    def result_copy(s):
        return remote(
            outbox.at[s], inbox.at[s - 1], res_send.at[s - 1], res_recv.at[s - 1],
            at(s, jnp.where(z + s >= ROW, over, l)),
        )

    def step(t, carry):
        s = jnp.where(z == 4, lax.rem(t + 4, 5), jnp.where(z == 5, lax.rem(t + 3, 5), t))
        s = jnp.where(z == 6, jnp.where(t == 0, 2, jnp.where(t < 3, t - 1, 7 - t)), s)
        s = jnp.where((z == 7) & (t < 2), 1 - t, s)

        chained = (z > 0) & (z < 5)

        @pl.when(chained & (t == jnp.where(z == 4, 2, 1)))
        def _():
            arrived(3)
            chain_copy(3).start()

        late_slot = ((s == 3) & ~chained) | (s == 4)

        @pl.when(late_slot | ((s == 2) & ((z == 0) | (z >= 6))) | ((s == 1) & ((z == 0) | (z == ROW - 1))))
        def _():
            arrived(s)

        block = slots[s]
        four = jnp.concatenate([block] * 4, 0)
        inner = by_layer(
            [lax.dot_general(cands[m], four, NT, preferred_element_type=jnp.float32) for m in range(LAYERS)]
        )
        v = smallest(base[...] - inner.astype(jnp.int32) * 1024)

        @pl.when(s == 0)
        def _():
            for k in range(16):
                keys[k : k + 1, :] = v[k][0:1, :]
                keys[16 + k : 17 + k, :] = v[k][4:5, :]

        @pl.when(s > 0)
        def _():
            for k in range(16):
                keys[31 - k : 32 - k, :] = v[k][0:1, :]
                keys[15 - k : 16 - k, :] = v[k][4:5, :]

        lanes = lax.broadcasted_iota(jnp.int32, (8, 128), 1)
        both = []
        for g in range(4):
            key = keys[8 * g : 8 * g + 8, :]
            place = key & 127
            which = (key >> 7) & 3
            found = [jnp.take_along_axis(table[a], place, axis=1, mode="promise_in_bounds") for a in range(4)]
            ident = jnp.where(
                which < 2, jnp.where(which == 0, found[0], found[1]), jnp.where(which == 2, found[2], found[3])
            )
            both.append(jnp.where(lanes < ROWS, key >> 9, pltpu.roll(ident, ROWS, 1)))
        for g in range(2):
            outbox[s, 8 * g : 8 * g + 8, :] = jnp.where(lanes < 64, both[g], pltpu.roll(both[g + 2], 64, 1))

        @pl.when(s > 0)
        def _():
            result_copy(s).start()

        return carry

    lax.fori_loop(0, STEPS + 1, step, 0)

    for s in range(1, STEPS + 1):
        @pl.when((z > 0) & (s - 1 + z < ROW))
        def _():
            chain_copy(s - 1).wait_send()

    for n, places in enumerate(((0, 2, 3), (0, 2, 3), (0, 2, 3), (0,))):

        @when_keeper(*places)
        def _():
            spread_copy(n, PARKED, 4, 4).wait_send()
            lower_copy(n, PARKED, 4, 4).wait_send()

    for k in (1, 2, 3):
        id_copy(k, l).wait_send()
    beside_copy(l).wait_send()
    for chunk in range(CAND_CHUNKS):
        across_copy(chunk, l).wait_send()
        onward_copy(chunk, l).wait_send()

    @pl.when(early)
    def _():
        park_copy().wait_send()

    def pair(x):
        whole = jnp.concatenate([x, pltpu.roll(x, 64, 1)], 0)
        return [whole, pltpu.roll(whole, 128 - ROWS, 1)]

    block = slots[0]
    own = lax.dot_general(ones, jnp.concatenate([block * block] * 4, 0), NT, preferred_element_type=jnp.float32)
    best = pair(outbox[0])
    for s in range(1, STEPS + 1):
        result_copy(s).wait_recv()
        best = merged(best, pair(inbox[s - 1]))
    dist = (best[0].astype(jnp.float32) + own[:K, :]) * (0.125 / D)
    both = jnp.concatenate([dist, best[1].astype(jnp.float32), dist, dist], 0).T
    out_ref[...] = both[:ROWS, :]
    for s in range(1, STEPS + 1):
        result_copy(s).wait_send()


def shards(queries, candidates, cand_ids):
    dma = pltpu.SemaphoreType.DMA
    any_space = pl.BlockSpec(memory_space=pltpu.HBM)
    vmem = pl.BlockSpec(memory_space=pltpu.VMEM)
    lists = pl.pallas_call(
        kernel,
        out_shape=jax.ShapeDtypeStruct((ROWS, 128), jnp.float32),
        in_specs=[any_space, any_space, any_space],
        out_specs=vmem,
        scratch_shapes=[
            pltpu.VMEM((PARKED + 4, ROWS, D), jnp.bfloat16),
            pltpu.VMEM((LAYERS, CB, D), jnp.bfloat16),
            pltpu.VMEM((LAYERS, 1, CB), jnp.int32),
            pltpu.VMEM((CB, 128), jnp.int32),
            pltpu.VMEM((4, 8, 128), jnp.int32),
            pltpu.VMEM((K, 128), jnp.int32),
            pltpu.VMEM((STEPS + 1, K // 2, 128), jnp.int32),
            pltpu.VMEM((STEPS, K // 2, 128), jnp.int32),
            dma((3,)),
            dma((STEPS,)),
            dma((PARKED + 4,)),
            dma,
            dma((8,)),
            dma((3, CAND_CHUNKS)),
            dma((3, CAND_CHUNKS)),
            dma((3,)),
            dma((3,)),
            dma((STEPS,)),
            dma((STEPS,)),
            pltpu.SemaphoreType.REGULAR((4,)),
        ],
        compiler_params=pltpu.CompilerParams(
            collective_id=0, has_side_effects=True, vmem_limit_bytes=16 * 1024 * 1024
        ),
    )(*(pltpu.with_memory_space_constraint(x, pltpu.HBM) for x in (queries, candidates, cand_ids.reshape(1, CB))))
    return lists[:, :K], lists[:, K : 2 * K].astype(jnp.int32)


def solution(mesh):
    return jax.shard_map(
        shards,
        mesh=mesh,
        in_specs=(P("loop", None), P(("loop", "layer"), None), P(("loop", "layer"))),
        out_specs=(P(("loop", "layer"), None), P(("loop", "layer"), None)),
        check_vma=False,
    )
```

```python
import jax
import jax.numpy as jnp
from jax import lax
from jax.experimental import pallas as pl
from jax.experimental.pallas import tpu as pltpu
from jax.sharding import PartitionSpec as P

D = 768
K = 32
STEPS = 4
LOOP = 64
ROW = 8
LAYERS = 4
CB = 128
ROWS = 32
PARKED = 5
CAND_CHUNKS = 4
CAND_PIECE = CB // CAND_CHUNKS
MESH = pl.DeviceIdType.MESH
NT = (((1,), (1,)), ((), ()))


def batcher(count):
    pairs = []
    p = 1
    while p < count:
        k = p
        while k >= 1:
            for j in range(k % p, count - k, 2 * k):
                for i in range(min(k, count - j - k)):
                    if (i + j) // (2 * p) == (i + j + k) // (2 * p):
                        pairs.append((i + j, i + j + k))
            k //= 2
        p *= 2
    return pairs


SORT16 = batcher(16)


def exchange(values, low, high):
    a, b = values[low], values[high]
    values[low], values[high] = jnp.minimum(a, b), jnp.maximum(a, b)


def settle(values):
    for gap in (8, 4, 2, 1):
        for k in range(16):
            if not k & gap:
                exchange(values, k, k + gap)


def smallest(key):
    row = lax.broadcasted_iota(jnp.int32, (8, 128), 0)
    upper = row >= 4
    v = [key[8 * g : 8 * g + 8, :] for g in range(16)]
    for low, high in SORT16:
        exchange(v, low, high)
    r = [pltpu.roll(v[15 - k], 4, 0) for k in range(16)]
    v = [jnp.where(upper, jnp.maximum(v[k], r[k]), jnp.minimum(v[k], r[k])) for k in range(16)]
    settle(v)
    for shift, lanes in ((2, 0), (3, 0), (4, 96), (4, 64)):
        r = [pltpu.roll(v[15 - k], shift, 0) for k in range(16)]
        if lanes:
            r = [pltpu.roll(x, lanes, 1) for x in r]
        v = [jnp.minimum(v[k], r[k]) for k in range(16)]
        r = [pltpu.roll(x, 4, 0) for x in v]
        v = [jnp.where(upper, jnp.maximum(v[k], r[k]), jnp.minimum(v[k], r[k])) for k in range(16)]
        settle(v)
    return v


def by_layer(parts):
    group = lax.broadcasted_iota(jnp.int32, parts[0].shape, 1) // ROWS
    return jnp.where(
        group < 2, jnp.where(group == 0, parts[0], parts[1]), jnp.where(group == 2, parts[2], parts[3])
    )


def merged(first, second):
    place = lax.broadcasted_iota(jnp.int32, (K, 128), 0)

    def before(a, b):
        return (a[0] < b[0]) | ((a[0] == b[0]) & (a[1] < b[1]))

    lower = before(first, second)
    now = [jnp.where(lower, a, b) for a, b in zip(first, second)]
    for gap in (16, 8, 4, 2, 1):
        head = (place & gap) == 0
        other = [jnp.where(head, pltpu.roll(x, K - gap, 0), pltpu.roll(x, gap, 0)) for x in now]
        keep = before(now, other) == head
        now = [jnp.where(keep, a, b) for a, b in zip(now, other)]
    return now


def kernel(
    q_ref, c_ref, id_ref, out_ref,
    slots, cands, idents, base, table, keys, outbox, inbox,
    local_sem, chain_send, slot_recv, park_send, spread_send, cand_send, cand_recv, id_send, id_recv,
    res_send, res_recv, ring_sem,
):
    i, l = lax.axis_index("loop"), lax.axis_index("layer")
    z = lax.rem(i, ROW)
    early = z < 4
    skew = (z == 1) | (z == 2)

    def at(offset, layer=l):
        return (lax.rem(i + offset + 2 * LOOP, LOOP), layer)

    over = l ^ 2
    keeper = (l & 1) == 1
    lower = l & 2

    def remote(src, dst, send, recv, device):
        return pltpu.make_async_remote_copy(
            src_ref=src, dst_ref=dst, send_sem=send, recv_sem=recv, device_id=device, device_id_type=MESH
        )

    own_rows = q_ref.at[pl.ds(l * ROWS, ROWS)]
    own_q = pltpu.make_async_copy(own_rows, slots.at[0], local_sem.at[0])
    own_c = pltpu.make_async_copy(c_ref, cands.at[l], local_sem.at[1])
    own_id = pltpu.make_async_copy(id_ref, idents.at[l], local_sem.at[2])

    barrier = pltpu.get_barrier_semaphore()

    def hello(device):
        pl.semaphore_signal(barrier, inc=1, device_id=device, device_id_type=MESH)

    def when_z(*places):
        hit = z == places[0]
        for place in places[1:]:
            hit = hit | (z == place)
        return pl.when(hit)

    def when_keeper(*places):
        hit = z == places[0]
        for place in places[1:]:
            hit = hit | (z == place)
        return pl.when(hit & keeper)

    @when_keeper(2, 3)
    def _():
        hello(at(ROW - 1, over))
        hello(at(ROW - 1, over ^ 1))

    @when_keeper(0, 3)
    def _():
        hello(at(ROW, over))
        hello(at(ROW, over ^ 1))

    @pl.when(z < ROW - 1)
    def _():
        hello(at(1))

    for place, late in ((0, (4, 5, 6, 7)), (2, (5, 6, 7)), (3, (6, 7))):

        @when_keeper(place)
        def _():
            for other in late:
                hello(at(other - place))
                hello(at(other - place, lower))

    @when_z(0)
    def _():
        hello(at(4))

    for k in (1, 2, 3):
        hello((i, l ^ k))
    own_q.start()
    own_id.start()
    own_c.start()
    expected = jnp.where(z == 0, 4, jnp.where(early, 5, jnp.where(z == 4, 6, jnp.where(z == 5, 6, 7))))
    pl.semaphore_wait(barrier, expected)

    def park_copy():
        slot = jnp.where(z == 2, PARKED + 1, PARKED) + jnp.where(keeper, 0, 2)
        device = at(jnp.where(skew, 1 - ROW, -ROW), over | 1)
        return remote(slots.at[0], slots.at[slot], park_send, slot_recv.at[slot], device)

    def first_copy():
        return remote(own_rows, slots.at[1], chain_send.at[0], slot_recv.at[1], at(-1))

    def chain_copy(s):
        return remote(slots.at[s], slots.at[s + 1], chain_send.at[s], slot_recv.at[s + 1], at(-1))

    def spread_copy(n, source, offset, slot):
        return remote(slots.at[source], slots.at[slot], spread_send.at[n], slot_recv.at[slot], at(offset))

    def lower_copy(n, source, offset, slot):
        return remote(
            slots.at[source + 2], slots.at[slot], spread_send.at[n + 4], slot_recv.at[slot], at(offset, lower)
        )

    def jump_copy():
        return remote(slots.at[0], slots.at[4], chain_send.at[4], slot_recv.at[4], at(-4))

    def arrived(slot):
        remote(slots.at[0], slots.at[slot], park_send, slot_recv.at[slot], at(1)).wait_recv()

    for late, places in ((4, (0,)), (5, (0, 2)), (6, (0, 2, 3)), (7, (0, 2, 3))):

        @when_z(late)
        def _():
            for place in places:
                pl.semaphore_signal(
                    ring_sem.at[late - 4], inc=1, device_id=at(place - late, l | 1), device_id_type=MESH
                )

    own_q.wait()

    @pl.when(early)
    def _():
        park_copy().start()

    @pl.when(z > 0)
    def _():
        first_copy().start()

    @when_z(4)
    def _():
        jump_copy().start()

    def across_copy(chunk, block):
        rows = pl.ds(chunk * CAND_PIECE, CAND_PIECE)
        return remote(
            c_ref.at[rows], cands.at[block, rows], cand_send.at[0, chunk], cand_recv.at[0, chunk], (i, l ^ 2)
        )

    def beside_copy(block):
        return remote(c_ref, cands.at[block], cand_send.at[1, 0], cand_recv.at[1, 0], (i, l ^ 1))

    def onward_copy(chunk, block):
        rows = pl.ds(chunk * CAND_PIECE, CAND_PIECE)
        return remote(
            cands.at[block, rows], cands.at[block, rows],
            cand_send.at[2, chunk], cand_recv.at[2, chunk], (i, l ^ 1),
        )

    def id_copy(k, block):
        return remote(id_ref, idents.at[block], id_send.at[k - 1], id_recv.at[k - 1], (i, l ^ k))

    for k in (1, 2, 3):
        id_copy(k, l).start()
    for chunk in range(CAND_CHUNKS):
        across_copy(chunk, l).start()
    beside_copy(l).start()

    @pl.when((z > 0) & (z < ROW - 1))
    def _():
        arrived(1)
        chain_copy(1).start()

    @when_keeper(0)
    def _():
        arrived(PARKED)
        arrived(PARKED + 2)
        for n, late in enumerate((7, 6, 5, 4)):
            pl.semaphore_wait(ring_sem.at[late - 4], 2)
            lower_copy(n, PARKED, late, 8 - late).start()
            spread_copy(n, PARKED, late, 8 - late).start()

    own_id.wait()
    for k in (1, 2, 3):
        id_copy(k, l ^ k).wait_recv()
    lane = lax.broadcasted_iota(jnp.int32, (CB, 128), 1)
    id_rows = [idents[m].astype(jnp.float32) for m in range(LAYERS)]
    id_cols = jnp.concatenate([jnp.broadcast_to(x, (ROWS, CB)) for x in id_rows], 0).T
    part = jnp.zeros((CB, 128), jnp.float32)
    for m in range(LAYERS):
        for k in range(4):
            shifted = pltpu.roll(jnp.broadcast_to(id_rows[m], (8, 128)), 32 * k, 1)[:1]
            part += jnp.where(shifted < id_cols, 1.0, 0.0)
    same = lax.broadcasted_iota(jnp.int32, (128, 128), 0) // ROWS == (
        lax.broadcasted_iota(jnp.int32, (128, 128), 1) // ROWS
    )
    rank = jnp.dot(
        part.astype(jnp.bfloat16),
        jnp.where(same, 1.0, 0.0).astype(jnp.bfloat16),
        preferred_element_type=jnp.float32,
    ).astype(jnp.int32)
    for a in range(4):
        total = jnp.zeros((1, 128), jnp.float32)
        for m in range(LAYERS):
            column = rank[:, ROWS * m : ROWS * m + 1]
            ident = id_cols[:, ROWS * m : ROWS * m + 1]
            total += jnp.sum(jnp.where(column == lane + 128 * a, ident, 0.0), 0, keepdims=True)
        table[a] = jnp.broadcast_to(total, (8, 128)).astype(jnp.int32)

    for chunk in range(CAND_CHUNKS):
        across_copy(chunk, l ^ 2).wait_recv()
        onward_copy(chunk, l ^ 2).start()

    @when_keeper(2)
    def _():
        for late in (5, 6, 7):
            pl.semaphore_wait(ring_sem.at[late - 4], 2)
        arrived(PARKED)
        arrived(PARKED + 2)
        for n, (offset, slot) in enumerate(((5, 2), (4, 3), (3, 4))):
            lower_copy(n, PARKED, offset, slot).start()
            spread_copy(n, PARKED, offset, slot).start()

    @when_keeper(3)
    def _():
        for late in (6, 7):
            pl.semaphore_wait(ring_sem.at[late - 4], 2)
        arrived(PARKED + 1)
        arrived(PARKED + 3)
        lower_copy(1, PARKED + 1, 4, 3).start()
        lower_copy(0, PARKED + 1, 3, 4).start()
        spread_copy(1, PARKED + 1, 4, 3).start()
        spread_copy(0, PARKED + 1, 3, 4).start()
        arrived(PARKED)
        spread_copy(2, PARKED, 4, 4).start()
        arrived(PARKED + 2)
        lower_copy(2, PARKED, 4, 4).start()

    @pl.when((z > 0) & (z < ROW - 2))
    def _():
        arrived(2)
        chain_copy(2).start()

    ones = jnp.ones((128, D), jnp.bfloat16)
    group = lax.broadcasted_iota(jnp.int32, (CB, 128), 1) // ROWS

    def norms(m, total):
        block = cands[m]
        found = lax.dot_general(block * block, ones, NT, preferred_element_type=jnp.float32)
        return jnp.where(group == m, found, total)

    own_c.wait()
    total = norms(l, jnp.zeros((CB, 128), jnp.float32))
    beside_copy(l ^ 1).wait_recv()
    total = norms(l ^ 2, norms(l ^ 1, total))
    for chunk in range(CAND_CHUNKS):
        onward_copy(chunk, l ^ 3).wait_recv()
    base[...] = norms(l ^ 3, total).astype(jnp.int32) * 512 + rank

    def result_copy(s):
        return remote(
            outbox.at[s], inbox.at[s - 1], res_send.at[s - 1], res_recv.at[s - 1],
            at(s, jnp.where(z + s >= ROW, over, l)),
        )

    def step(t, carry):
        s = jnp.where(z == 4, lax.rem(t + 4, 5), jnp.where(z == 5, lax.rem(t + 3, 5), t))
        s = jnp.where((z == 6) & (t < 3), jnp.where(t == 0, 2, t - 1), s)
        s = jnp.where((z == 7) & (t < 2), 1 - t, s)

        chained = (z > 1) & (z < 5)

        @pl.when(chained & (t == jnp.where(z == 4, 2, 1)))
        def _():
            arrived(3)
            chain_copy(3).start()

        late_slot = ((s == 3) & ~chained) | (s == 4)

        @pl.when(late_slot | ((s == 2) & ((z == 0) | (z >= 6))) | ((s == 1) & ((z == 0) | (z == ROW - 1))))
        def _():
            arrived(s)

        block = slots[s]
        four = jnp.concatenate([block] * 4, 0)
        inner = by_layer(
            [lax.dot_general(cands[m], four, NT, preferred_element_type=jnp.float32) for m in range(LAYERS)]
        )
        v = smallest(base[...] - inner.astype(jnp.int32) * 1024)

        @pl.when(s == 0)
        def _():
            for k in range(16):
                keys[k : k + 1, :] = v[k][0:1, :]
                keys[16 + k : 17 + k, :] = v[k][4:5, :]

        @pl.when(s > 0)
        def _():
            for k in range(16):
                keys[31 - k : 32 - k, :] = v[k][0:1, :]
                keys[15 - k : 16 - k, :] = v[k][4:5, :]

        group = lax.broadcasted_iota(jnp.int32, (8, 128), 1) // ROWS
        key = keys[0:8, :]
        for g in (1, 2, 3):
            key = jnp.where(group == g, pltpu.roll(keys[8 * g : 8 * g + 8, :], ROWS * g, 1), key)
        place = key & 127
        which = (key >> 7) & 3
        found = [jnp.take_along_axis(table[a], place, axis=1, mode="promise_in_bounds") for a in range(4)]
        outbox[s, 0:8, :] = key >> 9
        outbox[s, 8:16, :] = jnp.where(
            which < 2, jnp.where(which == 0, found[0], found[1]), jnp.where(which == 2, found[2], found[3])
        )

        @pl.when(s > 0)
        def _():
            result_copy(s).start()

        return carry

    lax.fori_loop(0, STEPS + 1, step, 0)

    for s in range(1, STEPS + 1):
        @pl.when((z > 0) & (s - 1 + z < ROW) & ((z > 1) | (s < 4)))
        def _():
            chain_copy(s - 1).wait_send()

    for n, places in enumerate(((0, 2, 3), (0, 2, 3), (0, 2, 3), (0,))):

        @when_keeper(*places)
        def _():
            spread_copy(n, PARKED, 4, 4).wait_send()
            lower_copy(n, PARKED, 4, 4).wait_send()

    for k in (1, 2, 3):
        id_copy(k, l).wait_send()
    beside_copy(l).wait_send()
    for chunk in range(CAND_CHUNKS):
        across_copy(chunk, l).wait_send()
        onward_copy(chunk, l).wait_send()

    @pl.when(early)
    def _():
        park_copy().wait_send()

    @when_z(4)
    def _():
        jump_copy().wait_send()

    for s in range(1, STEPS + 1):
        result_copy(s).wait_send()

    def pair(x):
        turns = [x] + [pltpu.roll(x, 128 - ROWS * g, 1) for g in (1, 2, 3)]
        return [jnp.concatenate([turn[h : h + 8] for turn in turns], 0) for h in (0, 8)]

    block = slots[0]
    own = lax.dot_general(ones, jnp.concatenate([block * block] * 4, 0), NT, preferred_element_type=jnp.float32)
    best = pair(outbox[0])
    for s in range(1, STEPS + 1):
        result_copy(s).wait_recv()
        best = merged(best, pair(inbox[s - 1]))
    dist = (best[0].astype(jnp.float32) + own[:K, :]) * (0.125 / D)
    both = jnp.concatenate([dist, best[1].astype(jnp.float32), dist, dist], 0).T
    out_ref[...] = both[:ROWS, :]


def shards(queries, candidates, cand_ids):
    dma = pltpu.SemaphoreType.DMA
    any_space = pl.BlockSpec(memory_space=pltpu.HBM)
    vmem = pl.BlockSpec(memory_space=pltpu.VMEM)
    lists = pl.pallas_call(
        kernel,
        out_shape=jax.ShapeDtypeStruct((ROWS, 128), jnp.float32),
        in_specs=[any_space, any_space, any_space],
        out_specs=vmem,
        scratch_shapes=[
            pltpu.VMEM((PARKED + 4, ROWS, D), jnp.bfloat16),
            pltpu.VMEM((LAYERS, CB, D), jnp.bfloat16),
            pltpu.VMEM((LAYERS, 1, CB), jnp.int32),
            pltpu.VMEM((CB, 128), jnp.int32),
            pltpu.VMEM((4, 8, 128), jnp.int32),
            pltpu.VMEM((K, 128), jnp.int32),
            pltpu.VMEM((STEPS + 1, K // 2, 128), jnp.int32),
            pltpu.VMEM((STEPS, K // 2, 128), jnp.int32),
            dma((3,)),
            dma((STEPS + 1,)),
            dma((PARKED + 4,)),
            dma,
            dma((8,)),
            dma((3, CAND_CHUNKS)),
            dma((3, CAND_CHUNKS)),
            dma((3,)),
            dma((3,)),
            dma((STEPS,)),
            dma((STEPS,)),
            pltpu.SemaphoreType.REGULAR((4,)),
        ],
        compiler_params=pltpu.CompilerParams(
            collective_id=0, has_side_effects=True, vmem_limit_bytes=16 * 1024 * 1024
        ),
    )(*(pltpu.with_memory_space_constraint(x, pltpu.HBM) for x in (queries, candidates, cand_ids.reshape(1, CB))))
    return lists[:, :K], lists[:, K : 2 * K].astype(jnp.int32)


def solution(mesh):
    return jax.shard_map(
        shards,
        mesh=mesh,
        in_specs=(P("loop", None), P(("loop", "layer"), None), P(("loop", "layer"))),
        out_specs=(P(("loop", "layer"), None), P(("loop", "layer"), None)),
        check_vma=False,
    )
```

```python
import jax
import jax.numpy as jnp
from jax import lax
from jax.experimental import pallas as pl
from jax.experimental.pallas import tpu as pltpu
from jax.sharding import PartitionSpec as P

D = 768
K = 32
STEPS = 4
LOOP = 64
ROW = 8
LAYERS = 4
CB = 128
ROWS = 32
PARKED = 5
CAND_PIECES = ((0, 48), (48, 32), (80, 32), (112, 16))
CAND_CHUNKS = len(CAND_PIECES)
MESH = pl.DeviceIdType.MESH
NT = (((1,), (1,)), ((), ()))


def batcher(count):
    pairs = []
    p = 1
    while p < count:
        k = p
        while k >= 1:
            for j in range(k % p, count - k, 2 * k):
                for i in range(min(k, count - j - k)):
                    if (i + j) // (2 * p) == (i + j + k) // (2 * p):
                        pairs.append((i + j, i + j + k))
            k //= 2
        p *= 2
    return pairs


SORT16 = batcher(16)


def exchange(values, low, high):
    a, b = values[low], values[high]
    values[low], values[high] = jnp.minimum(a, b), jnp.maximum(a, b)


def settle(values):
    for gap in (8, 4, 2, 1):
        for k in range(16):
            if not k & gap:
                exchange(values, k, k + gap)


def smallest(key):
    row = lax.broadcasted_iota(jnp.int32, (8, 128), 0)
    upper = row >= 4
    v = [key[8 * g : 8 * g + 8, :] for g in range(16)]
    for low, high in SORT16:
        exchange(v, low, high)
    r = [pltpu.roll(v[15 - k], 4, 0) for k in range(16)]
    v = [jnp.where(upper, jnp.maximum(v[k], r[k]), jnp.minimum(v[k], r[k])) for k in range(16)]
    settle(v)
    for shift, lanes in ((2, 0), (3, 0), (4, 96), (4, 64)):
        r = [pltpu.roll(v[15 - k], shift, 0) for k in range(16)]
        if lanes:
            r = [pltpu.roll(x, lanes, 1) for x in r]
        v = [jnp.minimum(v[k], r[k]) for k in range(16)]
        r = [pltpu.roll(x, 4, 0) for x in v]
        v = [jnp.where(upper, jnp.maximum(v[k], r[k]), jnp.minimum(v[k], r[k])) for k in range(16)]
        settle(v)
    return v


def by_layer(parts):
    group = lax.broadcasted_iota(jnp.int32, parts[0].shape, 1) // ROWS
    return jnp.where(
        group < 2, jnp.where(group == 0, parts[0], parts[1]), jnp.where(group == 2, parts[2], parts[3])
    )


def merged(first, second):
    place = lax.broadcasted_iota(jnp.int32, (K, 128), 0)

    def before(a, b):
        return (a[0] < b[0]) | ((a[0] == b[0]) & (a[1] < b[1]))

    lower = before(first, second)
    now = [jnp.where(lower, a, b) for a, b in zip(first, second)]
    for gap in (16, 8, 4, 2, 1):
        head = (place & gap) == 0
        other = [jnp.where(head, pltpu.roll(x, K - gap, 0), pltpu.roll(x, gap, 0)) for x in now]
        keep = before(now, other) == head
        now = [jnp.where(keep, a, b) for a, b in zip(now, other)]
    return now


def kernel(
    q_ref, c_ref, id_ref, out_ref,
    slots, cands, idents, base, table, keys, outbox, inbox,
    local_sem, chain_send, slot_recv, park_send, spread_send, cand_send, cand_recv, id_send, id_recv,
    res_send, res_recv, ring_sem,
):
    i, l = lax.axis_index("loop"), lax.axis_index("layer")
    z = lax.rem(i, ROW)
    early = z < 4
    skew = (z == 1) | (z == 2)

    def at(offset, layer=l):
        return (lax.rem(i + offset + 2 * LOOP, LOOP), layer)

    over = l ^ 2
    keeper = (l & 1) == 1
    lower = l & 2

    def remote(src, dst, send, recv, device):
        return pltpu.make_async_remote_copy(
            src_ref=src, dst_ref=dst, send_sem=send, recv_sem=recv, device_id=device, device_id_type=MESH
        )

    own_rows = q_ref.at[pl.ds(l * ROWS, ROWS)]
    own_q = pltpu.make_async_copy(own_rows, slots.at[0], local_sem.at[0])
    own_c = pltpu.make_async_copy(c_ref, cands.at[l], local_sem.at[1])
    own_id = pltpu.make_async_copy(id_ref, idents.at[l], local_sem.at[2])

    barrier = pltpu.get_barrier_semaphore()

    def hello(device):
        pl.semaphore_signal(barrier, inc=1, device_id=device, device_id_type=MESH)

    def when_z(*places):
        hit = z == places[0]
        for place in places[1:]:
            hit = hit | (z == place)
        return pl.when(hit)

    def when_keeper(*places):
        hit = z == places[0]
        for place in places[1:]:
            hit = hit | (z == place)
        return pl.when(hit & keeper)

    @when_keeper(2, 3)
    def _():
        hello(at(ROW - 1, over))
        hello(at(ROW - 1, over ^ 1))

    @when_keeper(0, 3)
    def _():
        hello(at(ROW, over))
        hello(at(ROW, over ^ 1))

    @pl.when(z < ROW - 1)
    def _():
        hello(at(1))

    for place, late in ((0, (4, 5, 6, 7)), (2, (5, 6, 7)), (3, (6, 7))):

        @when_keeper(place)
        def _():
            for other in late:
                hello(at(other - place))
                hello(at(other - place, lower))

    @when_z(0)
    def _():
        hello(at(4))

    for k in (1, 2, 3):
        hello((i, l ^ k))
    own_q.start()
    own_id.start()
    own_c.start()
    expected = jnp.where(z == 0, 4, jnp.where(early, 5, jnp.where(z == 4, 6, jnp.where(z == 5, 6, 7))))
    pl.semaphore_wait(barrier, expected)

    def park_copy():
        slot = jnp.where(z == 2, PARKED + 1, PARKED) + jnp.where(keeper, 0, 2)
        device = at(jnp.where(skew, 1 - ROW, -ROW), over | 1)
        return remote(slots.at[0], slots.at[slot], park_send, slot_recv.at[slot], device)

    def first_copy():
        return remote(own_rows, slots.at[1], chain_send.at[0], slot_recv.at[1], at(-1))

    def chain_copy(s):
        return remote(slots.at[s], slots.at[s + 1], chain_send.at[s], slot_recv.at[s + 1], at(-1))

    def spread_copy(n, source, offset, slot):
        return remote(slots.at[source], slots.at[slot], spread_send.at[n], slot_recv.at[slot], at(offset))

    def lower_copy(n, source, offset, slot):
        return remote(
            slots.at[source + 2], slots.at[slot], spread_send.at[n + 4], slot_recv.at[slot], at(offset, lower)
        )

    def jump_copy():
        return remote(slots.at[0], slots.at[4], chain_send.at[4], slot_recv.at[4], at(-4))

    def arrived(slot):
        remote(slots.at[0], slots.at[slot], park_send, slot_recv.at[slot], at(1)).wait_recv()

    for late, places in ((4, (0,)), (5, (0, 2)), (6, (0, 2, 3)), (7, (0, 2, 3))):

        @when_z(late)
        def _():
            for place in places:
                pl.semaphore_signal(
                    ring_sem.at[late - 4], inc=1, device_id=at(place - late, l | 1), device_id_type=MESH
                )

    own_q.wait()

    @pl.when(early)
    def _():
        park_copy().start()

    @pl.when(z > 0)
    def _():
        first_copy().start()

    @when_z(4)
    def _():
        jump_copy().start()

    def across_copy(chunk, block):
        rows = pl.ds(*CAND_PIECES[chunk])
        return remote(
            c_ref.at[rows], cands.at[block, rows], cand_send.at[0, chunk], cand_recv.at[0, chunk], (i, l ^ 2)
        )

    def beside_copy(block):
        return remote(c_ref, cands.at[block], cand_send.at[1, 0], cand_recv.at[1, 0], (i, l ^ 1))

    def onward_copy(chunk, block):
        rows = pl.ds(*CAND_PIECES[chunk])
        return remote(
            cands.at[block, rows], cands.at[block, rows],
            cand_send.at[2, chunk], cand_recv.at[2, chunk], (i, l ^ 1),
        )

    def id_copy(k, block):
        return remote(id_ref, idents.at[block], id_send.at[k - 1], id_recv.at[k - 1], (i, l ^ k))

    for k in (1, 2, 3):
        id_copy(k, l).start()
    for chunk in range(CAND_CHUNKS):
        across_copy(chunk, l).start()
    beside_copy(l).start()

    @pl.when((z > 0) & (z < ROW - 1))
    def _():
        arrived(1)
        chain_copy(1).start()

    @when_keeper(0)
    def _():
        arrived(PARKED)
        arrived(PARKED + 2)
        for n, late in enumerate((7, 6, 5, 4)):
            pl.semaphore_wait(ring_sem.at[late - 4], 2)
            lower_copy(n, PARKED, late, 8 - late).start()
            spread_copy(n, PARKED, late, 8 - late).start()

    own_id.wait()
    for k in (1, 2, 3):
        id_copy(k, l ^ k).wait_recv()
    lane = lax.broadcasted_iota(jnp.int32, (CB, 128), 1)
    id_rows = [idents[m].astype(jnp.float32) for m in range(LAYERS)]
    id_cols = jnp.concatenate([jnp.broadcast_to(x, (ROWS, CB)) for x in id_rows], 0).T
    part = jnp.zeros((CB, 128), jnp.float32)
    for m in range(LAYERS):
        for k in range(4):
            shifted = pltpu.roll(jnp.broadcast_to(id_rows[m], (8, 128)), 32 * k, 1)[:1]
            part += jnp.where(shifted < id_cols, 1.0, 0.0)
    same = lax.broadcasted_iota(jnp.int32, (128, 128), 0) // ROWS == (
        lax.broadcasted_iota(jnp.int32, (128, 128), 1) // ROWS
    )
    rank = jnp.dot(
        part.astype(jnp.bfloat16),
        jnp.where(same, 1.0, 0.0).astype(jnp.bfloat16),
        preferred_element_type=jnp.float32,
    ).astype(jnp.int32)
    for a in range(4):
        total = jnp.zeros((1, 128), jnp.float32)
        for m in range(LAYERS):
            column = rank[:, ROWS * m : ROWS * m + 1]
            ident = id_cols[:, ROWS * m : ROWS * m + 1]
            total += jnp.sum(jnp.where(column == lane + 128 * a, ident, 0.0), 0, keepdims=True)
        table[a] = jnp.broadcast_to(total, (8, 128)).astype(jnp.int32)

    for chunk in range(CAND_CHUNKS):
        across_copy(chunk, l ^ 2).wait_recv()
        onward_copy(chunk, l ^ 2).start()

    @when_keeper(2)
    def _():
        for late in (5, 6, 7):
            pl.semaphore_wait(ring_sem.at[late - 4], 2)
        arrived(PARKED)
        arrived(PARKED + 2)
        for n, (offset, slot) in enumerate(((5, 2), (4, 3), (3, 4))):
            lower_copy(n, PARKED, offset, slot).start()
            spread_copy(n, PARKED, offset, slot).start()

    @when_keeper(3)
    def _():
        for late in (6, 7):
            pl.semaphore_wait(ring_sem.at[late - 4], 2)
        arrived(PARKED + 1)
        arrived(PARKED + 3)
        lower_copy(1, PARKED + 1, 4, 3).start()
        lower_copy(0, PARKED + 1, 3, 4).start()
        spread_copy(1, PARKED + 1, 4, 3).start()
        spread_copy(0, PARKED + 1, 3, 4).start()
        arrived(PARKED)
        spread_copy(2, PARKED, 4, 4).start()
        arrived(PARKED + 2)
        lower_copy(2, PARKED, 4, 4).start()

    @pl.when((z > 0) & (z < ROW - 2))
    def _():
        arrived(2)
        chain_copy(2).start()

    ones = jnp.ones((128, D), jnp.bfloat16)
    group = lax.broadcasted_iota(jnp.int32, (CB, 128), 1) // ROWS

    def norms(m, total):
        block = cands[m]
        found = lax.dot_general(block * block, ones, NT, preferred_element_type=jnp.float32)
        return jnp.where(group == m, found, total)

    own_c.wait()
    total = norms(l, jnp.zeros((CB, 128), jnp.float32))
    beside_copy(l ^ 1).wait_recv()
    total = norms(l ^ 2, norms(l ^ 1, total))
    for chunk in range(CAND_CHUNKS):
        onward_copy(chunk, l ^ 3).wait_recv()
    base[...] = norms(l ^ 3, total).astype(jnp.int32) * 512 + rank

    def result_copy(s):
        return remote(
            outbox.at[s], inbox.at[s - 1], res_send.at[s - 1], res_recv.at[s - 1],
            at(s, jnp.where(z + s >= ROW, over, l)),
        )

    def step(t, carry):
        s = jnp.where(z == 4, lax.rem(t + 4, 5), jnp.where(z == 5, lax.rem(t + 3, 5), t))
        s = jnp.where((z == 6) & (t < 3), jnp.where(t == 0, 2, t - 1), s)
        s = jnp.where((z == 7) & (t < 2), 1 - t, s)

        chained = (z > 1) & (z < 5)

        @pl.when(chained & (t == jnp.where(z == 4, 2, 1)))
        def _():
            arrived(3)
            chain_copy(3).start()

        late_slot = ((s == 3) & ~chained) | (s == 4)

        @pl.when(late_slot | ((s == 2) & ((z == 0) | (z >= 6))) | ((s == 1) & ((z == 0) | (z == ROW - 1))))
        def _():
            arrived(s)

        block = slots[s]
        four = jnp.concatenate([block] * 4, 0)
        inner = by_layer(
            [lax.dot_general(cands[m], four, NT, preferred_element_type=jnp.float32) for m in range(LAYERS)]
        )
        v = smallest(base[...] - inner.astype(jnp.int32) * 1024)

        @pl.when(s == 0)
        def _():
            for k in range(16):
                keys[k : k + 1, :] = v[k][0:1, :]
                keys[16 + k : 17 + k, :] = v[k][4:5, :]

        @pl.when(s > 0)
        def _():
            for k in range(16):
                keys[31 - k : 32 - k, :] = v[k][0:1, :]
                keys[15 - k : 16 - k, :] = v[k][4:5, :]

        group = lax.broadcasted_iota(jnp.int32, (8, 128), 1) // ROWS
        key = keys[0:8, :]
        for g in (1, 2, 3):
            key = jnp.where(group == g, pltpu.roll(keys[8 * g : 8 * g + 8, :], ROWS * g, 1), key)
        place = key & 127
        which = (key >> 7) & 3
        found = [jnp.take_along_axis(table[a], place, axis=1, mode="promise_in_bounds") for a in range(4)]
        outbox[s, 0:8, :] = key >> 9
        outbox[s, 8:16, :] = jnp.where(
            which < 2, jnp.where(which == 0, found[0], found[1]), jnp.where(which == 2, found[2], found[3])
        )

        @pl.when(s > 0)
        def _():
            result_copy(s).start()

        return carry

    lax.fori_loop(0, STEPS + 1, step, 0)

    for s in range(1, STEPS + 1):
        @pl.when((z > 0) & (s - 1 + z < ROW) & ((z > 1) | (s < 4)))
        def _():
            chain_copy(s - 1).wait_send()

    for n, places in enumerate(((0, 2, 3), (0, 2, 3), (0, 2, 3), (0,))):

        @when_keeper(*places)
        def _():
            spread_copy(n, PARKED, 4, 4).wait_send()
            lower_copy(n, PARKED, 4, 4).wait_send()

    for k in (1, 2, 3):
        id_copy(k, l).wait_send()
    beside_copy(l).wait_send()
    for chunk in range(CAND_CHUNKS):
        across_copy(chunk, l).wait_send()
        onward_copy(chunk, l).wait_send()

    @pl.when(early)
    def _():
        park_copy().wait_send()

    @when_z(4)
    def _():
        jump_copy().wait_send()

    for s in range(1, STEPS + 1):
        result_copy(s).wait_send()

    def pair(x):
        turns = [x] + [pltpu.roll(x, 128 - ROWS * g, 1) for g in (1, 2, 3)]
        return [jnp.concatenate([turn[h : h + 8] for turn in turns], 0) for h in (0, 8)]

    block = slots[0]
    own = lax.dot_general(ones, jnp.concatenate([block * block] * 4, 0), NT, preferred_element_type=jnp.float32)
    best = pair(outbox[0])
    for s in range(1, STEPS + 1):
        result_copy(s).wait_recv()
        best = merged(best, pair(inbox[s - 1]))
    dist = (best[0].astype(jnp.float32) + own[:K, :]) * (0.125 / D)
    both = jnp.concatenate([dist, best[1].astype(jnp.float32), dist, dist], 0).T
    out_ref[...] = both[:ROWS, :]


def shards(queries, candidates, cand_ids):
    dma = pltpu.SemaphoreType.DMA
    any_space = pl.BlockSpec(memory_space=pltpu.HBM)
    vmem = pl.BlockSpec(memory_space=pltpu.VMEM)
    lists = pl.pallas_call(
        kernel,
        out_shape=jax.ShapeDtypeStruct((ROWS, 128), jnp.float32),
        in_specs=[any_space, any_space, any_space],
        out_specs=vmem,
        scratch_shapes=[
            pltpu.VMEM((PARKED + 4, ROWS, D), jnp.bfloat16),
            pltpu.VMEM((LAYERS, CB, D), jnp.bfloat16),
            pltpu.VMEM((LAYERS, 1, CB), jnp.int32),
            pltpu.VMEM((CB, 128), jnp.int32),
            pltpu.VMEM((4, 8, 128), jnp.int32),
            pltpu.VMEM((K, 128), jnp.int32),
            pltpu.VMEM((STEPS + 1, K // 2, 128), jnp.int32),
            pltpu.VMEM((STEPS, K // 2, 128), jnp.int32),
            dma((3,)),
            dma((STEPS + 1,)),
            dma((PARKED + 4,)),
            dma,
            dma((8,)),
            dma((3, CAND_CHUNKS)),
            dma((3, CAND_CHUNKS)),
            dma((3,)),
            dma((3,)),
            dma((STEPS,)),
            dma((STEPS,)),
            pltpu.SemaphoreType.REGULAR((4,)),
        ],
        compiler_params=pltpu.CompilerParams(
            collective_id=0, has_side_effects=True, vmem_limit_bytes=16 * 1024 * 1024
        ),
    )(*(pltpu.with_memory_space_constraint(x, pltpu.HBM) for x in (queries, candidates, cand_ids.reshape(1, CB))))
    return lists[:, :K], lists[:, K : 2 * K].astype(jnp.int32)


def solution(mesh):
    return jax.shard_map(
        shards,
        mesh=mesh,
        in_specs=(P("loop", None), P(("loop", "layer"), None), P(("loop", "layer"))),
        out_specs=(P(("loop", "layer"), None), P(("loop", "layer"), None)),
        check_vma=False,
    )
```

```python
import jax
import jax.numpy as jnp
from jax import lax
from jax.experimental import pallas as pl
from jax.experimental.pallas import tpu as pltpu
from jax.sharding import PartitionSpec as P

D = 768
K = 32
STEPS = 4
LOOP = 64
ROW = 8
LAYERS = 4
CB = 128
ROWS = 32
PARKED = 5
CAND_PIECES = ((0, 48), (48, 32), (80, 32), (112, 16))
CAND_CHUNKS = len(CAND_PIECES)
MESH = pl.DeviceIdType.MESH
NT = (((1,), (1,)), ((), ()))


def batcher(count):
    pairs = []
    p = 1
    while p < count:
        k = p
        while k >= 1:
            for j in range(k % p, count - k, 2 * k):
                for i in range(min(k, count - j - k)):
                    if (i + j) // (2 * p) == (i + j + k) // (2 * p):
                        pairs.append((i + j, i + j + k))
            k //= 2
        p *= 2
    return pairs


SORT16 = batcher(16)


def exchange(values, low, high):
    a, b = values[low], values[high]
    values[low], values[high] = jnp.minimum(a, b), jnp.maximum(a, b)


def settle(values):
    for gap in (8, 4, 2, 1):
        for k in range(16):
            if not k & gap:
                exchange(values, k, k + gap)


def smallest(key):
    row = lax.broadcasted_iota(jnp.int32, (8, 128), 0)
    upper = row >= 4
    v = [key[8 * g : 8 * g + 8, :] for g in range(16)]
    for low, high in SORT16:
        exchange(v, low, high)
    r = [pltpu.roll(v[15 - k], 4, 0) for k in range(16)]
    v = [jnp.where(upper, jnp.maximum(v[k], r[k]), jnp.minimum(v[k], r[k])) for k in range(16)]
    settle(v)
    for shift, lanes in ((2, 0), (3, 0), (4, 96), (4, 64)):
        r = [pltpu.roll(v[15 - k], shift, 0) for k in range(16)]
        if lanes:
            r = [pltpu.roll(x, lanes, 1) for x in r]
        v = [jnp.minimum(v[k], r[k]) for k in range(16)]
        r = [pltpu.roll(x, 4, 0) for x in v]
        v = [jnp.where(upper, jnp.maximum(v[k], r[k]), jnp.minimum(v[k], r[k])) for k in range(16)]
        settle(v)
    return v


def by_layer(parts):
    group = lax.broadcasted_iota(jnp.int32, parts[0].shape, 1) // ROWS
    return jnp.where(
        group < 2, jnp.where(group == 0, parts[0], parts[1]), jnp.where(group == 2, parts[2], parts[3])
    )


def merged(first, second):
    place = lax.broadcasted_iota(jnp.int32, (K, 128), 0)

    def before(a, b):
        return (a[0] < b[0]) | ((a[0] == b[0]) & (a[1] < b[1]))

    lower = before(first, second)
    now = [jnp.where(lower, a, b) for a, b in zip(first, second)]
    for gap in (16, 8, 4, 2, 1):
        head = (place & gap) == 0
        other = [jnp.where(head, pltpu.roll(x, K - gap, 0), pltpu.roll(x, gap, 0)) for x in now]
        keep = before(now, other) == head
        now = [jnp.where(keep, a, b) for a, b in zip(now, other)]
    return now


def kernel(
    q_ref, c_ref, id_ref, out_ref,
    slots, cands, idents, base, table, keys, outbox, inbox,
    local_sem, chain_send, slot_recv, park_send, spread_send, cand_send, cand_recv, id_send, id_recv,
    res_send, res_recv, ring_sem,
):
    i, l = lax.axis_index("loop"), lax.axis_index("layer")
    z = lax.rem(i, ROW)
    early = z < 4
    skew = (z == 1) | (z == 2)

    def at(offset, layer=l):
        return (lax.rem(i + offset + 2 * LOOP, LOOP), layer)

    over = l ^ 2
    keeper = (l & 1) == 1
    lower = l & 2

    def remote(src, dst, send, recv, device):
        return pltpu.make_async_remote_copy(
            src_ref=src, dst_ref=dst, send_sem=send, recv_sem=recv, device_id=device, device_id_type=MESH
        )

    own_rows = q_ref.at[pl.ds(l * ROWS, ROWS)]
    own_q = pltpu.make_async_copy(own_rows, slots.at[0], local_sem.at[0])
    own_c = pltpu.make_async_copy(c_ref, cands.at[l], local_sem.at[1])
    own_id = pltpu.make_async_copy(id_ref, idents.at[l], local_sem.at[2])

    barrier = pltpu.get_barrier_semaphore()

    def hello(device):
        pl.semaphore_signal(barrier, inc=1, device_id=device, device_id_type=MESH)

    def when_z(*places):
        hit = z == places[0]
        for place in places[1:]:
            hit = hit | (z == place)
        return pl.when(hit)

    def when_keeper(*places):
        hit = z == places[0]
        for place in places[1:]:
            hit = hit | (z == place)
        return pl.when(hit & keeper)

    @when_keeper(2, 3)
    def _():
        hello(at(ROW - 1, over))
        hello(at(ROW - 1, over ^ 1))

    @when_keeper(0, 3)
    def _():
        hello(at(ROW, over))
        hello(at(ROW, over ^ 1))

    @pl.when(z < ROW - 1)
    def _():
        hello(at(1))

    for place, late in ((0, (4, 5, 6, 7)), (2, (5, 6, 7)), (3, (6, 7))):

        @when_keeper(place)
        def _():
            for other in late:
                hello(at(other - place))
                hello(at(other - place, lower))

    @when_z(0)
    def _():
        hello(at(4))

    for k in (1, 2, 3):
        hello((i, l ^ k))
    own_q.start()
    own_id.start()
    own_c.start()
    expected = jnp.where(z == 0, 4, jnp.where(early, 5, jnp.where(z == 4, 6, jnp.where(z == 5, 6, 7))))
    pl.semaphore_wait(barrier, expected)

    def park_copy():
        slot = jnp.where(z == 2, PARKED + 1, PARKED) + jnp.where(keeper, 0, 2)
        device = at(jnp.where(skew, 1 - ROW, -ROW), over | 1)
        return remote(slots.at[0], slots.at[slot], park_send, slot_recv.at[slot], device)

    def first_copy():
        return remote(own_rows, slots.at[1], chain_send.at[0], slot_recv.at[1], at(-1))

    def chain_copy(s):
        return remote(slots.at[s], slots.at[s + 1], chain_send.at[s], slot_recv.at[s + 1], at(-1))

    def spread_copy(n, source, offset, slot):
        return remote(slots.at[source], slots.at[slot], spread_send.at[n], slot_recv.at[slot], at(offset))

    def lower_copy(n, source, offset, slot):
        return remote(
            slots.at[source + 2], slots.at[slot], spread_send.at[n + 4], slot_recv.at[slot], at(offset, lower)
        )

    def jump_copy():
        return remote(slots.at[0], slots.at[4], chain_send.at[4], slot_recv.at[4], at(-4))

    def arrived(slot):
        remote(slots.at[0], slots.at[slot], park_send, slot_recv.at[slot], at(1)).wait_recv()

    for late, places in ((4, (0,)), (5, (0, 2)), (6, (0, 2, 3)), (7, (0, 2, 3))):

        @when_z(late)
        def _():
            for place in places:
                pl.semaphore_signal(
                    ring_sem.at[late - 4], inc=1, device_id=at(place - late, l | 1), device_id_type=MESH
                )

    def across_copy(chunk, block):
        rows = pl.ds(*CAND_PIECES[chunk])
        return remote(
            c_ref.at[rows], cands.at[block, rows], cand_send.at[0, chunk], cand_recv.at[0, chunk], (i, l ^ 2)
        )

    def beside_copy(block):
        return remote(c_ref, cands.at[block], cand_send.at[1, 0], cand_recv.at[1, 0], (i, l ^ 1))

    def onward_copy(chunk, block):
        rows = pl.ds(*CAND_PIECES[chunk])
        return remote(
            cands.at[block, rows], cands.at[block, rows],
            cand_send.at[2, chunk], cand_recv.at[2, chunk], (i, l ^ 1),
        )

    def id_copy(k, block):
        return remote(id_ref, idents.at[block], id_send.at[k - 1], id_recv.at[k - 1], (i, l ^ k))

    def offer():
        for k in (1, 2, 3):
            id_copy(k, l).start()
        for chunk in range(CAND_CHUNKS):
            across_copy(chunk, l).start()

    @pl.when(~early)
    def _():
        offer()

    own_q.wait()

    @pl.when(early)
    def _():
        park_copy().start()

    @pl.when(z > 0)
    def _():
        first_copy().start()

    @when_z(4)
    def _():
        jump_copy().start()

    @pl.when(early)
    def _():
        offer()

    beside_copy(l).start()

    @pl.when((z > 0) & (z < ROW - 1))
    def _():
        arrived(1)
        chain_copy(1).start()

    @when_keeper(0)
    def _():
        arrived(PARKED)
        arrived(PARKED + 2)
        for n, late in enumerate((7, 6, 5, 4)):
            pl.semaphore_wait(ring_sem.at[late - 4], 2)
            lower_copy(n, PARKED, late, 8 - late).start()
            spread_copy(n, PARKED, late, 8 - late).start()

    own_id.wait()
    for k in (1, 2, 3):
        id_copy(k, l ^ k).wait_recv()
    lane = lax.broadcasted_iota(jnp.int32, (CB, 128), 1)
    id_rows = [idents[m].astype(jnp.float32) for m in range(LAYERS)]
    id_cols = jnp.concatenate([jnp.broadcast_to(x, (ROWS, CB)) for x in id_rows], 0).T
    part = jnp.zeros((CB, 128), jnp.float32)
    for m in range(LAYERS):
        for k in range(4):
            shifted = pltpu.roll(jnp.broadcast_to(id_rows[m], (8, 128)), 32 * k, 1)[:1]
            part += jnp.where(shifted < id_cols, 1.0, 0.0)
    same = lax.broadcasted_iota(jnp.int32, (128, 128), 0) // ROWS == (
        lax.broadcasted_iota(jnp.int32, (128, 128), 1) // ROWS
    )
    rank = jnp.dot(
        part.astype(jnp.bfloat16),
        jnp.where(same, 1.0, 0.0).astype(jnp.bfloat16),
        preferred_element_type=jnp.float32,
    ).astype(jnp.int32)
    for a in range(4):
        total = jnp.zeros((1, 128), jnp.float32)
        for m in range(LAYERS):
            column = rank[:, ROWS * m : ROWS * m + 1]
            ident = id_cols[:, ROWS * m : ROWS * m + 1]
            total += jnp.sum(jnp.where(column == lane + 128 * a, ident, 0.0), 0, keepdims=True)
        table[a] = jnp.broadcast_to(total, (8, 128)).astype(jnp.int32)

    for chunk in range(CAND_CHUNKS):
        across_copy(chunk, l ^ 2).wait_recv()
        onward_copy(chunk, l ^ 2).start()

    @when_keeper(2)
    def _():
        for late in (5, 6, 7):
            pl.semaphore_wait(ring_sem.at[late - 4], 2)
        arrived(PARKED)
        arrived(PARKED + 2)
        for n, (offset, slot) in enumerate(((5, 2), (4, 3), (3, 4))):
            lower_copy(n, PARKED, offset, slot).start()
            spread_copy(n, PARKED, offset, slot).start()

    @when_keeper(3)
    def _():
        for late in (6, 7):
            pl.semaphore_wait(ring_sem.at[late - 4], 2)
        arrived(PARKED + 1)
        arrived(PARKED + 3)
        lower_copy(1, PARKED + 1, 4, 3).start()
        lower_copy(0, PARKED + 1, 3, 4).start()
        spread_copy(1, PARKED + 1, 4, 3).start()
        spread_copy(0, PARKED + 1, 3, 4).start()
        arrived(PARKED)
        spread_copy(2, PARKED, 4, 4).start()
        arrived(PARKED + 2)
        lower_copy(2, PARKED, 4, 4).start()

    @pl.when((z > 0) & (z < ROW - 2))
    def _():
        arrived(2)
        chain_copy(2).start()

    ones = jnp.ones((128, D), jnp.bfloat16)
    group = lax.broadcasted_iota(jnp.int32, (CB, 128), 1) // ROWS

    def norms(m, total):
        block = cands[m]
        found = lax.dot_general(block * block, ones, NT, preferred_element_type=jnp.float32)
        return jnp.where(group == m, found, total)

    own_c.wait()
    total = norms(l, jnp.zeros((CB, 128), jnp.float32))
    beside_copy(l ^ 1).wait_recv()
    total = norms(l ^ 2, norms(l ^ 1, total))
    for chunk in range(CAND_CHUNKS):
        onward_copy(chunk, l ^ 3).wait_recv()
    base[...] = norms(l ^ 3, total).astype(jnp.int32) * 512 + rank

    def result_copy(s):
        return remote(
            outbox.at[s], inbox.at[s - 1], res_send.at[s - 1], res_recv.at[s - 1],
            at(s, jnp.where(z + s >= ROW, over, l)),
        )

    def step(t, carry):
        s = jnp.where(z == 4, lax.rem(t + 4, 5), jnp.where(z == 5, lax.rem(t + 3, 5), t))
        s = jnp.where((z == 6) & (t < 3), jnp.where(t == 0, 2, t - 1), s)
        s = jnp.where((z == 7) & (t < 2), 1 - t, s)

        chained = (z > 1) & (z < 5)

        @pl.when(chained & (t == jnp.where(z == 4, 2, 1)))
        def _():
            arrived(3)
            chain_copy(3).start()

        late_slot = ((s == 3) & ~chained) | (s == 4)

        @pl.when(late_slot | ((s == 2) & ((z == 0) | (z >= 6))) | ((s == 1) & ((z == 0) | (z == ROW - 1))))
        def _():
            arrived(s)

        block = slots[s]
        four = jnp.concatenate([block] * 4, 0)
        inner = by_layer(
            [lax.dot_general(cands[m], four, NT, preferred_element_type=jnp.float32) for m in range(LAYERS)]
        )
        v = smallest(base[...] - inner.astype(jnp.int32) * 1024)

        @pl.when(s == 0)
        def _():
            for k in range(16):
                keys[k : k + 1, :] = v[k][0:1, :]
                keys[16 + k : 17 + k, :] = v[k][4:5, :]

        @pl.when(s > 0)
        def _():
            for k in range(16):
                keys[31 - k : 32 - k, :] = v[k][0:1, :]
                keys[15 - k : 16 - k, :] = v[k][4:5, :]

        group = lax.broadcasted_iota(jnp.int32, (8, 128), 1) // ROWS
        key = keys[0:8, :]
        for g in (1, 2, 3):
            key = jnp.where(group == g, pltpu.roll(keys[8 * g : 8 * g + 8, :], ROWS * g, 1), key)
        place = key & 127
        which = (key >> 7) & 3
        found = [jnp.take_along_axis(table[a], place, axis=1, mode="promise_in_bounds") for a in range(4)]
        outbox[s, 0:8, :] = key >> 9
        outbox[s, 8:16, :] = jnp.where(
            which < 2, jnp.where(which == 0, found[0], found[1]), jnp.where(which == 2, found[2], found[3])
        )

        @pl.when(s > 0)
        def _():
            result_copy(s).start()

        return carry

    lax.fori_loop(0, STEPS + 1, step, 0)

    for s in range(1, STEPS + 1):
        @pl.when((z > 0) & (s - 1 + z < ROW) & ((z > 1) | (s < 4)))
        def _():
            chain_copy(s - 1).wait_send()

    for n, places in enumerate(((0, 2, 3), (0, 2, 3), (0, 2, 3), (0,))):

        @when_keeper(*places)
        def _():
            spread_copy(n, PARKED, 4, 4).wait_send()
            lower_copy(n, PARKED, 4, 4).wait_send()

    for k in (1, 2, 3):
        id_copy(k, l).wait_send()
    beside_copy(l).wait_send()
    for chunk in range(CAND_CHUNKS):
        across_copy(chunk, l).wait_send()
        onward_copy(chunk, l).wait_send()

    @pl.when(early)
    def _():
        park_copy().wait_send()

    @when_z(4)
    def _():
        jump_copy().wait_send()

    for s in range(1, STEPS + 1):
        result_copy(s).wait_send()

    def pair(x):
        turns = [x] + [pltpu.roll(x, 128 - ROWS * g, 1) for g in (1, 2, 3)]
        return [jnp.concatenate([turn[h : h + 8] for turn in turns], 0) for h in (0, 8)]

    block = slots[0]
    own = lax.dot_general(ones, jnp.concatenate([block * block] * 4, 0), NT, preferred_element_type=jnp.float32)
    best = pair(outbox[0])
    for s in range(1, STEPS + 1):
        result_copy(s).wait_recv()
        best = merged(best, pair(inbox[s - 1]))
    dist = (best[0].astype(jnp.float32) + own[:K, :]) * (0.125 / D)
    both = jnp.concatenate([dist, best[1].astype(jnp.float32), dist, dist], 0).T
    out_ref[...] = both[:ROWS, :]


def shards(queries, candidates, cand_ids):
    dma = pltpu.SemaphoreType.DMA
    any_space = pl.BlockSpec(memory_space=pltpu.HBM)
    vmem = pl.BlockSpec(memory_space=pltpu.VMEM)
    lists = pl.pallas_call(
        kernel,
        out_shape=jax.ShapeDtypeStruct((ROWS, 128), jnp.float32),
        in_specs=[any_space, any_space, any_space],
        out_specs=vmem,
        scratch_shapes=[
            pltpu.VMEM((PARKED + 4, ROWS, D), jnp.bfloat16),
            pltpu.VMEM((LAYERS, CB, D), jnp.bfloat16),
            pltpu.VMEM((LAYERS, 1, CB), jnp.int32),
            pltpu.VMEM((CB, 128), jnp.int32),
            pltpu.VMEM((4, 8, 128), jnp.int32),
            pltpu.VMEM((K, 128), jnp.int32),
            pltpu.VMEM((STEPS + 1, K // 2, 128), jnp.int32),
            pltpu.VMEM((STEPS, K // 2, 128), jnp.int32),
            dma((3,)),
            dma((STEPS + 1,)),
            dma((PARKED + 4,)),
            dma,
            dma((8,)),
            dma((3, CAND_CHUNKS)),
            dma((3, CAND_CHUNKS)),
            dma((3,)),
            dma((3,)),
            dma((STEPS,)),
            dma((STEPS,)),
            pltpu.SemaphoreType.REGULAR((4,)),
        ],
        compiler_params=pltpu.CompilerParams(
            collective_id=0, has_side_effects=True, vmem_limit_bytes=16 * 1024 * 1024
        ),
    )(*(pltpu.with_memory_space_constraint(x, pltpu.HBM) for x in (queries, candidates, cand_ids.reshape(1, CB))))
    return lists[:, :K], lists[:, K : 2 * K].astype(jnp.int32)


def solution(mesh):
    return jax.shard_map(
        shards,
        mesh=mesh,
        in_specs=(P("loop", None), P(("loop", "layer"), None), P(("loop", "layer"))),
        out_specs=(P(("loop", "layer"), None), P(("loop", "layer"), None)),
        check_vma=False,
    )
```

```python
import jax
import jax.numpy as jnp
from jax import lax
from jax.experimental import pallas as pl
from jax.experimental.pallas import tpu as pltpu
from jax.sharding import PartitionSpec as P

D = 768
K = 32
STEPS = 4
LOOP = 64
ROW = 8
LAYERS = 4
CB = 128
ROWS = 32
PARKED = 5
CAND_PIECES = ((0, 48), (48, 32), (80, 32), (112, 16))
CAND_CHUNKS = len(CAND_PIECES)
MESH = pl.DeviceIdType.MESH
NT = (((1,), (1,)), ((), ()))


def batcher(count):
    pairs = []
    p = 1
    while p < count:
        k = p
        while k >= 1:
            for j in range(k % p, count - k, 2 * k):
                for i in range(min(k, count - j - k)):
                    if (i + j) // (2 * p) == (i + j + k) // (2 * p):
                        pairs.append((i + j, i + j + k))
            k //= 2
        p *= 2
    return pairs


SORT16 = batcher(16)


def exchange(values, low, high):
    a, b = values[low], values[high]
    values[low], values[high] = jnp.minimum(a, b), jnp.maximum(a, b)


def settle(values):
    for gap in (8, 4, 2, 1):
        for k in range(16):
            if not k & gap:
                exchange(values, k, k + gap)


def smallest(key):
    row = lax.broadcasted_iota(jnp.int32, (8, 128), 0)
    upper = row >= 4
    v = [key[8 * g : 8 * g + 8, :] for g in range(16)]
    for low, high in SORT16:
        exchange(v, low, high)
    r = [pltpu.roll(v[15 - k], 4, 0) for k in range(16)]
    v = [jnp.where(upper, jnp.maximum(v[k], r[k]), jnp.minimum(v[k], r[k])) for k in range(16)]
    settle(v)
    for shift, lanes in ((2, 0), (3, 0), (4, 96), (4, 64)):
        r = [pltpu.roll(v[15 - k], shift, 0) for k in range(16)]
        if lanes:
            r = [pltpu.roll(x, lanes, 1) for x in r]
        v = [jnp.minimum(v[k], r[k]) for k in range(16)]
        r = [pltpu.roll(x, 4, 0) for x in v]
        v = [jnp.where(upper, jnp.maximum(v[k], r[k]), jnp.minimum(v[k], r[k])) for k in range(16)]
        settle(v)
    return v


def by_layer(parts):
    group = lax.broadcasted_iota(jnp.int32, parts[0].shape, 1) // ROWS
    return jnp.where(
        group < 2, jnp.where(group == 0, parts[0], parts[1]), jnp.where(group == 2, parts[2], parts[3])
    )


def merged(first, second):
    place = lax.broadcasted_iota(jnp.int32, (K, 128), 0)

    def before(a, b):
        return (a[0] < b[0]) | ((a[0] == b[0]) & (a[1] < b[1]))

    lower = before(first, second)
    now = [jnp.where(lower, a, b) for a, b in zip(first, second)]
    for gap in (16, 8, 4, 2, 1):
        head = (place & gap) == 0
        other = [jnp.where(head, pltpu.roll(x, K - gap, 0), pltpu.roll(x, gap, 0)) for x in now]
        keep = before(now, other) == head
        now = [jnp.where(keep, a, b) for a, b in zip(now, other)]
    return now


def kernel(
    q_ref, c_ref, id_ref, out_ref,
    slots, cands, idents, base, table, keys, outbox, inbox,
    local_sem, chain_send, slot_recv, park_send, spread_send, cand_send, cand_recv, id_send, id_recv,
    res_send, res_recv, ring_sem,
):
    i, l = lax.axis_index("loop"), lax.axis_index("layer")
    z = lax.rem(i, ROW)
    early = z < 4
    skew = (z == 1) | (z == 2)

    def at(offset, layer=l):
        return (lax.rem(i + offset + 2 * LOOP, LOOP), layer)

    over = l ^ 2
    keeper = (l & 1) == 1
    lower = l & 2

    def remote(src, dst, send, recv, device):
        return pltpu.make_async_remote_copy(
            src_ref=src, dst_ref=dst, send_sem=send, recv_sem=recv, device_id=device, device_id_type=MESH
        )

    own_rows = q_ref.at[pl.ds(l * ROWS, ROWS)]
    own_q = pltpu.make_async_copy(own_rows, slots.at[0], local_sem.at[0])
    own_c = pltpu.make_async_copy(c_ref, cands.at[l], local_sem.at[1])
    own_id = pltpu.make_async_copy(id_ref, idents.at[l], local_sem.at[2])

    barrier = pltpu.get_barrier_semaphore()

    def hello(device):
        pl.semaphore_signal(barrier, inc=1, device_id=device, device_id_type=MESH)

    def when_z(*places):
        hit = z == places[0]
        for place in places[1:]:
            hit = hit | (z == place)
        return pl.when(hit)

    def when_keeper(*places):
        hit = z == places[0]
        for place in places[1:]:
            hit = hit | (z == place)
        return pl.when(hit & keeper)

    @when_keeper(2, 3)
    def _():
        hello(at(ROW - 1, over))
        hello(at(ROW - 1, over ^ 1))

    @when_keeper(0, 3)
    def _():
        hello(at(ROW, over))
        hello(at(ROW, over ^ 1))

    @pl.when(z < ROW - 1)
    def _():
        hello(at(1))

    for place, late in ((0, (4, 5, 6, 7)), (2, (5, 6, 7)), (3, (6, 7))):

        @when_keeper(place)
        def _():
            for other in late:
                hello(at(other - place))
                hello(at(other - place, lower))

    @when_z(0)
    def _():
        hello(at(4))

    for k in (1, 2, 3):
        hello((i, l ^ k))
    own_q.start()
    own_id.start()
    own_c.start()
    expected = jnp.where(z == 0, 4, jnp.where(early, 5, jnp.where(z == 4, 6, jnp.where(z == 5, 6, 7))))
    pl.semaphore_wait(barrier, expected)

    def park_copy():
        slot = jnp.where(z == 2, PARKED + 1, PARKED) + jnp.where(keeper, 0, 2)
        device = at(jnp.where(skew, 1 - ROW, -ROW), over | 1)
        return remote(slots.at[0], slots.at[slot], park_send, slot_recv.at[slot], device)

    def first_copy():
        return remote(own_rows, slots.at[1], chain_send.at[0], slot_recv.at[1], at(-1))

    def chain_copy(s):
        return remote(slots.at[s], slots.at[s + 1], chain_send.at[s], slot_recv.at[s + 1], at(-1))

    def spread_copy(n, source, offset, slot):
        return remote(slots.at[source], slots.at[slot], spread_send.at[n], slot_recv.at[slot], at(offset))

    def lower_copy(n, source, offset, slot):
        return remote(
            slots.at[source + 2], slots.at[slot], spread_send.at[n + 4], slot_recv.at[slot], at(offset, lower)
        )

    def jump_copy():
        return remote(slots.at[0], slots.at[4], chain_send.at[4], slot_recv.at[4], at(-4))

    def arrived(slot):
        remote(slots.at[0], slots.at[slot], park_send, slot_recv.at[slot], at(1)).wait_recv()

    for late, places in ((4, (0,)), (5, (0, 2)), (6, (0, 2, 3)), (7, (0, 2, 3))):

        @when_z(late)
        def _():
            for place in places:
                pl.semaphore_signal(
                    ring_sem.at[late - 4], inc=1, device_id=at(place - late, l | 1), device_id_type=MESH
                )

    def across_copy(chunk, block):
        rows = pl.ds(*CAND_PIECES[chunk])
        return remote(
            c_ref.at[rows], cands.at[block, rows], cand_send.at[0, chunk], cand_recv.at[0, chunk], (i, l ^ 2)
        )

    def beside_copy(block):
        return remote(c_ref, cands.at[block], cand_send.at[1, 0], cand_recv.at[1, 0], (i, l ^ 1))

    def onward_copy(chunk, block):
        rows = pl.ds(*CAND_PIECES[chunk])
        return remote(
            cands.at[block, rows], cands.at[block, rows],
            cand_send.at[2, chunk], cand_recv.at[2, chunk], (i, l ^ 1),
        )

    def id_copy(k, block):
        return remote(id_ref, idents.at[block], id_send.at[k - 1], id_recv.at[k - 1], (i, l ^ k))

    def offer():
        for k in (1, 2, 3):
            id_copy(k, l).start()
        for chunk in range(CAND_CHUNKS):
            across_copy(chunk, l).start()

    @pl.when(~early)
    def _():
        offer()

    own_q.wait()

    @pl.when(early)
    def _():
        park_copy().start()

    @pl.when(z > 0)
    def _():
        first_copy().start()

    @when_z(4)
    def _():
        jump_copy().start()

    @pl.when(early)
    def _():
        offer()

    beside_copy(l).start()

    @pl.when((z > 0) & (z < ROW - 1))
    def _():
        arrived(1)
        chain_copy(1).start()

    @when_keeper(0)
    def _():
        arrived(PARKED)
        arrived(PARKED + 2)
        for n, late in enumerate((7, 6, 5, 4)):
            pl.semaphore_wait(ring_sem.at[late - 4], 2)
            lower_copy(n, PARKED, late, 8 - late).start()
            spread_copy(n, PARKED, late, 8 - late).start()

    own_id.wait()
    for k in (1, 2, 3):
        id_copy(k, l ^ k).wait_recv()
    lane = lax.broadcasted_iota(jnp.int32, (CB, 128), 1)
    id_rows = [idents[m].astype(jnp.float32) for m in range(LAYERS)]
    id_cols = jnp.concatenate([jnp.broadcast_to(x, (ROWS, CB)) for x in id_rows], 0).T
    part = jnp.zeros((CB, 128), jnp.float32)
    for m in range(LAYERS):
        for k in range(4):
            shifted = pltpu.roll(jnp.broadcast_to(id_rows[m], (8, 128)), 32 * k, 1)[:1]
            part += jnp.where(shifted < id_cols, 1.0, 0.0)
    same = lax.broadcasted_iota(jnp.int32, (128, 128), 0) // ROWS == (
        lax.broadcasted_iota(jnp.int32, (128, 128), 1) // ROWS
    )
    rank = jnp.dot(
        part.astype(jnp.bfloat16),
        jnp.where(same, 1.0, 0.0).astype(jnp.bfloat16),
        preferred_element_type=jnp.float32,
    ).astype(jnp.int32)
    for a in range(4):
        total = jnp.zeros((1, 128), jnp.float32)
        for m in range(LAYERS):
            column = rank[:, ROWS * m : ROWS * m + 1]
            ident = id_cols[:, ROWS * m : ROWS * m + 1]
            total += jnp.sum(jnp.where(column == lane + 128 * a, ident, 0.0), 0, keepdims=True)
        table[a] = jnp.broadcast_to(total, (8, 128)).astype(jnp.int32)

    for chunk in range(CAND_CHUNKS):
        across_copy(chunk, l ^ 2).wait_recv()
        onward_copy(chunk, l ^ 2).start()

    @when_keeper(2)
    def _():
        for late in (5, 6, 7):
            pl.semaphore_wait(ring_sem.at[late - 4], 2)
        arrived(PARKED)
        arrived(PARKED + 2)
        for n, (offset, slot) in enumerate(((5, 2), (4, 3), (3, 4))):
            lower_copy(n, PARKED, offset, slot).start()
            spread_copy(n, PARKED, offset, slot).start()

    @when_keeper(3)
    def _():
        for late in (6, 7):
            pl.semaphore_wait(ring_sem.at[late - 4], 2)
        arrived(PARKED + 1)
        arrived(PARKED + 3)
        lower_copy(1, PARKED + 1, 4, 3).start()
        lower_copy(0, PARKED + 1, 3, 4).start()
        spread_copy(1, PARKED + 1, 4, 3).start()
        spread_copy(0, PARKED + 1, 3, 4).start()
        arrived(PARKED)
        spread_copy(2, PARKED, 4, 4).start()
        arrived(PARKED + 2)
        lower_copy(2, PARKED, 4, 4).start()

    @pl.when((z > 0) & (z < ROW - 2))
    def _():
        arrived(2)
        chain_copy(2).start()

    ones = jnp.ones((128, D), jnp.bfloat16)
    group = lax.broadcasted_iota(jnp.int32, (CB, 128), 1) // ROWS

    def norms(m, total):
        block = cands[m]
        found = lax.dot_general(block * block, ones, NT, preferred_element_type=jnp.float32)
        return jnp.where(group == m, found, total)

    own_c.wait()
    total = norms(l, jnp.zeros((CB, 128), jnp.float32))
    beside_copy(l ^ 1).wait_recv()
    total = norms(l ^ 2, norms(l ^ 1, total))
    for chunk in range(CAND_CHUNKS):
        onward_copy(chunk, l ^ 3).wait_recv()
    base[...] = norms(l ^ 3, total).astype(jnp.int32) * 512 + rank

    def result_copy(s):
        return remote(
            outbox.at[s], inbox.at[s - 1], res_send.at[s - 1], res_recv.at[s - 1],
            at(s, jnp.where(z + s >= ROW, over, l)),
        )

    def step(t, carry):
        s = jnp.where(z == 4, lax.rem(t + 4, 5), jnp.where(z == 5, lax.rem(t + 3, 5), t))
        s = jnp.where((z == 6) & (t < 3), jnp.where(t == 0, 2, t - 1), s)
        s = jnp.where((z == 7) & (t < 2), 1 - t, s)

        chained = (z > 1) & (z < 5)

        @pl.when(chained & (t == jnp.where(z == 4, 2, 1)))
        def _():
            arrived(3)
            chain_copy(3).start()

        late_slot = ((s == 3) & ~chained) | (s == 4)

        @pl.when(late_slot | ((s == 2) & ((z == 0) | (z >= 6))) | ((s == 1) & ((z == 0) | (z == ROW - 1))))
        def _():
            arrived(s)

        block = slots[s]
        four = jnp.concatenate([block] * 4, 0)
        every = lax.dot_general(cands[...].reshape(LAYERS * CB, D), four, NT, preferred_element_type=jnp.float32)
        inner = by_layer([every[CB * m : CB * m + CB] for m in range(LAYERS)])
        v = smallest(base[...] - inner.astype(jnp.int32) * 1024)

        @pl.when(s == 0)
        def _():
            for k in range(16):
                keys[k : k + 1, :] = v[k][0:1, :]
                keys[16 + k : 17 + k, :] = v[k][4:5, :]

        @pl.when(s > 0)
        def _():
            for k in range(16):
                keys[31 - k : 32 - k, :] = v[k][0:1, :]
                keys[15 - k : 16 - k, :] = v[k][4:5, :]

        group = lax.broadcasted_iota(jnp.int32, (8, 128), 1) // ROWS
        key = keys[0:8, :]
        for g in (1, 2, 3):
            key = jnp.where(group == g, pltpu.roll(keys[8 * g : 8 * g + 8, :], ROWS * g, 1), key)
        place = key & 127
        which = (key >> 7) & 3
        found = [jnp.take_along_axis(table[a], place, axis=1, mode="promise_in_bounds") for a in range(4)]
        outbox[s, 0:8, :] = key >> 9
        outbox[s, 8:16, :] = jnp.where(
            which < 2, jnp.where(which == 0, found[0], found[1]), jnp.where(which == 2, found[2], found[3])
        )

        @pl.when(s > 0)
        def _():
            result_copy(s).start()

        return carry

    lax.fori_loop(0, STEPS + 1, step, 0)

    for s in range(1, STEPS + 1):
        @pl.when((z > 0) & (s - 1 + z < ROW) & ((z > 1) | (s < 4)))
        def _():
            chain_copy(s - 1).wait_send()

    for n, places in enumerate(((0, 2, 3), (0, 2, 3), (0, 2, 3), (0,))):

        @when_keeper(*places)
        def _():
            spread_copy(n, PARKED, 4, 4).wait_send()
            lower_copy(n, PARKED, 4, 4).wait_send()

    for k in (1, 2, 3):
        id_copy(k, l).wait_send()
    beside_copy(l).wait_send()
    for chunk in range(CAND_CHUNKS):
        across_copy(chunk, l).wait_send()
        onward_copy(chunk, l).wait_send()

    @pl.when(early)
    def _():
        park_copy().wait_send()

    @when_z(4)
    def _():
        jump_copy().wait_send()

    for s in range(1, STEPS + 1):
        result_copy(s).wait_send()

    def pair(x):
        turns = [x] + [pltpu.roll(x, 128 - ROWS * g, 1) for g in (1, 2, 3)]
        return [jnp.concatenate([turn[h : h + 8] for turn in turns], 0) for h in (0, 8)]

    block = slots[0]
    own = lax.dot_general(ones, jnp.concatenate([block * block] * 4, 0), NT, preferred_element_type=jnp.float32)
    best = pair(outbox[0])
    for s in range(1, STEPS + 1):
        result_copy(s).wait_recv()
        best = merged(best, pair(inbox[s - 1]))
    dist = (best[0].astype(jnp.float32) + own[:K, :]) * (0.125 / D)
    both = jnp.concatenate([dist, best[1].astype(jnp.float32), dist, dist], 0).T
    out_ref[...] = both[:ROWS, :]


def shards(queries, candidates, cand_ids):
    dma = pltpu.SemaphoreType.DMA
    any_space = pl.BlockSpec(memory_space=pltpu.HBM)
    vmem = pl.BlockSpec(memory_space=pltpu.VMEM)
    lists = pl.pallas_call(
        kernel,
        out_shape=jax.ShapeDtypeStruct((ROWS, 128), jnp.float32),
        in_specs=[any_space, any_space, any_space],
        out_specs=vmem,
        scratch_shapes=[
            pltpu.VMEM((PARKED + 4, ROWS, D), jnp.bfloat16),
            pltpu.VMEM((LAYERS, CB, D), jnp.bfloat16),
            pltpu.VMEM((LAYERS, 1, CB), jnp.int32),
            pltpu.VMEM((CB, 128), jnp.int32),
            pltpu.VMEM((4, 8, 128), jnp.int32),
            pltpu.VMEM((K, 128), jnp.int32),
            pltpu.VMEM((STEPS + 1, K // 2, 128), jnp.int32),
            pltpu.VMEM((STEPS, K // 2, 128), jnp.int32),
            dma((3,)),
            dma((STEPS + 1,)),
            dma((PARKED + 4,)),
            dma,
            dma((8,)),
            dma((3, CAND_CHUNKS)),
            dma((3, CAND_CHUNKS)),
            dma((3,)),
            dma((3,)),
            dma((STEPS,)),
            dma((STEPS,)),
            pltpu.SemaphoreType.REGULAR((4,)),
        ],
        compiler_params=pltpu.CompilerParams(
            collective_id=0, has_side_effects=True, vmem_limit_bytes=16 * 1024 * 1024
        ),
    )(*(pltpu.with_memory_space_constraint(x, pltpu.HBM) for x in (queries, candidates, cand_ids.reshape(1, CB))))
    return lists[:, :K], lists[:, K : 2 * K].astype(jnp.int32)


def solution(mesh):
    return jax.shard_map(
        shards,
        mesh=mesh,
        in_specs=(P("loop", None), P(("loop", "layer"), None), P(("loop", "layer"))),
        out_specs=(P(("loop", "layer"), None), P(("loop", "layer"), None)),
        check_vma=False,
    )
```
